256 devices in a mesh: tm: 16 (over y, x), slab: 16 (over z, core).
Axes of the slice: x: 4, y: 4, z: 8, core: 2. Of those that a mesh axis runs over, the one named last changes fastest.
Arguments:
- increments: float32 [16, 768, 8, 768], P('tm', 'slab'), may hold values from -6 to 6
- courant: float32 [16, 768, 2, 768], P('tm', 'slab'), may hold values from -0.4 to 0.4
- deviation: float32 [768, 8, 768], P('slab'), may hold values from 0.5 to 2
- spectrum: float32 [768, 768], P(None, 'slab'), may hold values from 0.02 to 1
- observed_cells: int32 [16, 131072], P('tm', 'slab'), may hold values from 0 to 294911
- innovation: float32 [16, 131072], P('tm', 'slab'), may hold values from -6 to 6
- error_weights: float32 [16, 131072], P('tm', 'slab'), may hold values from 0.5 to 4
Outputs:
- gradient: float32 [16, 768, 8, 768], P('tm', 'slab')
The draws below stay inside these ranges and needn't reach their ends.
Inputs may be any that keep to these rules, and one draw needn't show every extreme that they name: `observed_cells`: entry s * 8192 + o of a subwindow's row indexes a cell of latitude slab s, numbered row-major over (row in the slab, vertical value, column); a cell may be observed more than once.
All inputs are finite; a program needn't handle non-finite values.
Results may differ from the reference program's by a relative error of at most 0.00005.
Values sent between devices are 32-bit elements; how exact they have to be, the bound alone decides.
No kernel may reach another device: no remote copies, remote signals or barrier semaphores. Data moves between devices by JAX's collectives and lax.ppermute only.
A program may use at most 64 MiB of HBM per device.

```python
import math
import jax
import jax.numpy as jnp
from jax import lax

VERT = 8
LAT = 768
LON = 768
STEPS = 4
OBS_DEV = 8192
SUBW = 16
N_SLAB = 16


def place_ends(drawn, stream_key, smallest, top_value):
    dims = drawn.shape
    spot = [jax.random.randint(jax.random.fold_in(stream_key, axis), (), 0, dims[axis]) for axis in range(len(dims))]
    drawn = drawn.at[tuple(spot)].set(smallest)
    longest = dims.index(max(dims))
    spot[longest] = (spot[longest] + 1) % dims[longest]
    return drawn.at[tuple(spot)].set(top_value)


def steps_of(key, shape, cuts, least, high):
    gain, own = 1.0, jax.random.fold_in(key, 6)
    for axis_at, blocks in cuts:
        heights = jnp.exp(jax.random.uniform(jax.random.fold_in(own, axis_at), (blocks,), jnp.float32, least / len(cuts), high / len(cuts)))
        gain = gain * jnp.repeat(heights, shape[axis_at] // blocks).reshape([-1 if axis == axis_at else 1 for axis in range(len(shape))])
    return gain


def normal_values(key, shape, scale, limit, shards=(), kind=jnp.bfloat16):
    result = scale * jax.random.normal(key, shape, jnp.float32)
    if shards:
        result = result * steps_of(key, shape, shards, -0.22, 0.18)
    return jnp.clip(result, -limit, limit).astype(kind)


def setup_inputs(seed: int = 0) -> dict:
    key_list = jax.random.split(jax.random.key(seed), 8)
    return {
        "increments": normal_values(key_list[0], (SUBW, LAT, VERT, LON), 1.0, 6.0, ((0, 16), (1, 16)), jnp.float32),
        "courant": jnp.clip(jax.random.uniform(key_list[1], (SUBW, LAT, 2, LON), jnp.float32, -0.4, 0.4) * steps_of(key_list[1], (SUBW, LAT, 2, LON), ((0, 16), (1, 16)), -0.4, 0.0), -0.4, 0.4),
        "deviation": jnp.clip(jnp.exp(math.log(2.0) - 1.3862944 * jax.random.uniform(key_list[2], (LAT, VERT, LON), jnp.float32) ** steps_of(key_list[2], (LAT, VERT, LON), ((0, 16),), -0.2, 0.2)), 0.5, 2.0),
        "spectrum": jnp.clip(jnp.exp(math.log(1.0) - 3.912023 * jax.random.uniform(key_list[3], (LAT, LON), jnp.float32) ** steps_of(key_list[3], (LAT, LON), ((1, 16),), -0.2, 0.2)), 0.02, 1.0),
        "observed_cells": place_ends(jax.random.randint(key_list[4], (SUBW, N_SLAB * OBS_DEV), 0, (LAT // N_SLAB) * VERT * LON), jax.random.fold_in(key_list[4], 1), 0, ((LAT // N_SLAB) * VERT * LON) - 1).astype(jnp.int32),
        "innovation": normal_values(key_list[5], (SUBW, N_SLAB * OBS_DEV), 1.0, 6.0, ((0, 16), (1, 16)), jnp.float32),
        "error_weights": jnp.clip(jnp.exp(math.log(4.0) - 2.0794415 * jax.random.uniform(key_list[6], (SUBW, N_SLAB * OBS_DEV), jnp.float32) ** steps_of(key_list[6], (SUBW, N_SLAB * OBS_DEV), ((0, 16), (1, 16)), -0.2, 0.2)), 0.5, 4.0),
    }


DIFFUSION = 0.1
PRECISE = lax.Precision.HIGHEST

def hartley_table(length):
    index = jnp.arange(length, dtype=jnp.int32)
    phase = index[:, None] * index[None, :] % length
    angle = phase.astype(jnp.float32) * (2.0 * math.pi / length)
    return ((jnp.cos(angle) + jnp.sin(angle)) / math.sqrt(length)).astype(jnp.float32)

def cosine_table(length):
    index = jnp.arange(length, dtype=jnp.int32)
    phase = (2 * index[None, :] + 1) * index[:, None] % (4 * length)
    angle = phase.astype(jnp.float32) * (math.pi / (2 * length))
    scales = jnp.where(index == 0, math.sqrt(1.0 / length), math.sqrt(2.0 / length)).astype(jnp.float32)
    return (scales[:, None] * jnp.cos(angle)).astype(jnp.float32)

def tangent_step(state, winds):
    eastern = jnp.roll(state, -1, axis=2)
    western = jnp.roll(state, 1, axis=2)
    padded = jnp.pad(state, ((1, 1), (0, 0), (0, 0)))
    northern = padded[2:]
    southern = padded[:-2]
    zonal = winds[:, 0:1, :]
    meridional = winds[:, 1:2, :]
    spread = DIFFUSION * (northern + southern + eastern + western - 4.0 * state)
    return state + spread - 0.5 * zonal * (eastern - western) - 0.5 * meridional * (northern - southern)

def reference(increments, courant, deviation, spectrum, observed_cells, innovation, error_weights):

    def observe(state, cells):
        flat = state.reshape(N_SLAB, -1)
        return jnp.take_along_axis(flat, cells.reshape(N_SLAB, -1), axis=1).reshape(-1)

    def trajectory(forcing):

        def advance(carry, inputs):
            state = carry + inputs[0]
            for step_index in range(STEPS):
                state = tangent_step(state, inputs[1])
            return (state, observe(state, inputs[2]))
        final, seen = lax.scan(advance, jnp.zeros_like(forcing[0]), (forcing, courant, observed_cells))
        return seen
    seen, pullback = jax.vjp(trajectory, increments)
    adjoint, = pullback(error_weights * (seen - innovation))
    zonal_table = hartley_table(LON)
    merid_table = cosine_table(LAT)

    def covariance(field):
        scaled = deviation * field
        zonal = jnp.dot(scaled.reshape(-1, LON), zonal_table, preferred_element_type=jnp.float32, precision=PRECISE)
        merid = jnp.dot(merid_table, zonal.reshape(LAT, -1), preferred_element_type=jnp.float32, precision=PRECISE)
        merid = merid.reshape(LAT, VERT, LON) * spectrum[:, None, :]
        back = jnp.dot(merid_table.T, merid.reshape(LAT, -1), preferred_element_type=jnp.float32, precision=PRECISE)
        zonal_back = jnp.dot(back.reshape(-1, LON), zonal_table, preferred_element_type=jnp.float32, precision=PRECISE)
        return deviation * zonal_back.reshape(LAT, VERT, LON)
    return increments + lax.map(covariance, adjoint)
```

```python
import functools
import math

import jax
import jax.numpy as jnp
import numpy as np
from jax import lax
from jax.experimental import pallas as pl
from jax.experimental.pallas import tpu as pltpu
from jax.sharding import PartitionSpec as P

STEPS = 4
GROUP = 8
HALO = 32
ROWS = 48
FRAME = ROWS + 2 * HALO
PAD = 8
PACKED = 160
F32 = jnp.float32
BF16 = jnp.bfloat16


def split_table(table):
    high = table.astype(jnp.bfloat16)
    low = (table - high.astype(np.float64)).astype(jnp.bfloat16)
    return np.stack([high, low])


def hartley_table(length):
    index = np.arange(length)
    angle = (index[:, None] * index[None, :] % length) * (2.0 * math.pi / length)
    return (np.cos(angle) + np.sin(angle)) / math.sqrt(length)


def cosine_table(length):
    index = np.arange(length)
    angle = ((2 * index[None, :] + 1) * index[:, None] % (4 * length)) * (math.pi / (2 * length))
    scales = np.where(index == 0, math.sqrt(1.0 / length), math.sqrt(2.0 / length))
    return scales[:, None] * np.cos(angle)


def params(megabytes, grid=True):
    return pltpu.CompilerParams(
        vmem_limit_bytes=megabytes * 1024 * 1024,
        dimension_semantics=("arbitrary",) if grid else None,
    )


def cost(flops, size):
    return pl.CostEstimate(flops=flops, bytes_accessed=size, transcendentals=0)


def whole(shape):
    return pl.BlockSpec(shape, lambda *_: (0,) * len(shape))


def packed_place(i):
    pair = lax.shift_right_logical(i, 1)
    depth = 32 - 8 * pair
    offset = 64 * pair - 8 * pair * (pair - 1) + (i & 1) * depth
    return pair, depth, offset


def rows8(start):
    return pl.ds(pl.multiple_of(start, 8), 8)


def scatter_kernel(row_ref, col_ref, w_ref, z_ref, out_ref, acc):
    step = pl.program_id(0)
    rows, cols = acc.shape[1], acc.shape[2]
    count = row_ref.shape[-1]

    @pl.when(step == 0)
    def _():
        acc[...] = jnp.zeros_like(acc)

    row_iota = lax.broadcasted_iota(jnp.int32, (rows, count), 0)
    col_iota = lax.broadcasted_iota(jnp.int32, (cols, count), 0)
    at_row = jnp.where(row_iota == row_ref[0], 1.0, 0.0).astype(BF16)
    at_col = jnp.where(col_iota == col_ref[0], 1.0, 0.0).astype(BF16)
    for which, ref in enumerate((w_ref, z_ref)):
        value = ref[0]
        high = value.astype(BF16)
        low = (value - high.astype(F32)).astype(BF16)
        for part in (high, low):
            acc[which] += lax.dot_general(
                at_row * part, at_col, (((1,), (1,)), ((), ())), preferred_element_type=F32
            )

    @pl.when(step == pl.num_programs(0) - 1)
    def _():
        for v in range(rows // ROWS):
            for which in range(2):
                out_ref[v, which] = acc[which, v * ROWS : (v + 1) * ROWS, :]


def scatter(cells, weights, innovation, vertical, columns):
    count = cells.shape[0]
    chunk = 1024
    line = cells // columns
    col = cells - line * columns
    row = (line % vertical) * ROWS + line // vertical
    shape = (count // chunk, 1, chunk)
    spec = pl.BlockSpec((1, 1, chunk), lambda i: (i, 0, 0))
    out = (vertical, 2, ROWS, columns)
    return pl.pallas_call(
        scatter_kernel,
        grid=(count // chunk,),
        in_specs=[spec] * 4,
        out_specs=whole(out),
        out_shape=jax.ShapeDtypeStruct(out, F32),
        scratch_shapes=[pltpu.VMEM((2, vertical * ROWS, columns), F32)],
        compiler_params=params(40),
        cost_estimate=cost(2 * 4 * count * vertical * ROWS * columns, 4 << 20),
        name="observation_maps",
    )(
        row.reshape(shape),
        col.reshape(shape),
        weights.reshape(shape),
        (weights * innovation).reshape(shape),
    )


def pack_kernel(skip, reverse, info, data_ref, up_ref, down_ref):
    k = pl.program_id(0)
    pair, depth, offset = packed_place(GROUP - 1 - k if reverse else k)
    for m in range(4):

        @pl.when(m < 4 - pair)
        def _():
            up_ref[:, rows8(offset + depth - 8 * (m + 1)), :] = data_ref[
                0, skip:, ROWS - 8 * (m + 1) : ROWS - 8 * m, :
            ]
            down_ref[:, rows8(offset + 8 * m), :] = data_ref[0, skip:, 8 * m : 8 * m + 8, :]


def pack(info, data, skip, reverse):
    parts, columns = data.shape[1], data.shape[3]
    out = (parts - skip, PACKED, columns)
    return pl.pallas_call(
        functools.partial(pack_kernel, skip, reverse),
        grid_spec=pltpu.PrefetchScalarGridSpec(
            num_scalar_prefetch=1,
            grid=(GROUP,),
            in_specs=[
                pl.BlockSpec((1, parts, ROWS, columns), lambda k, info: (k ^ info[0], 0, 0, 0))
            ],
            out_specs=[whole(out), whole(out)],
        ),
        out_shape=[jax.ShapeDtypeStruct(out, F32)] * 2,
        compiler_params=params(24),
        cost_estimate=cost(0, 6 << 20),
        name="pack_adjoint_halo" if reverse else "pack_halo",
    )(info, data)


def forcing_kernel(info, maps_ref, end_ref, out_ref, up_ref, down_ref):
    k = pl.program_id(0)
    pair, depth, offset = packed_place(GROUP - 1 - k)
    forcing = maps_ref[0, 0] * end_ref[0] - maps_ref[0, 1]
    out_ref[0] = forcing
    for m in range(4):

        @pl.when(m < 4 - pair)
        def _():
            up_ref[rows8(offset + depth - 8 * (m + 1)), :] = forcing[
                ROWS - 8 * (m + 1) : ROWS - 8 * m, :
            ]
            down_ref[rows8(offset + 8 * m), :] = forcing[8 * m : 8 * m + 8, :]


def forcing_of(info, maps, ends):
    columns = ends.shape[2]
    out = (PACKED, columns)
    block = pl.BlockSpec((1, ROWS, columns), lambda k, info: (k, 0, 0))
    return pl.pallas_call(
        forcing_kernel,
        grid_spec=pltpu.PrefetchScalarGridSpec(
            num_scalar_prefetch=1,
            grid=(GROUP,),
            in_specs=[
                pl.BlockSpec((1, 2, ROWS, columns), lambda k, info: (k ^ info[0], 0, 0, 0)),
                block,
            ],
            out_specs=[block, whole(out), whole(out)],
        ),
        out_shape=[jax.ShapeDtypeStruct(ends.shape, F32)]
        + [jax.ShapeDtypeStruct(out, F32)] * 2,
        compiler_params=params(16),
        cost_estimate=cost(1 << 20, 6 << 20),
        name="forcing",
    )(info, maps, ends)


def start_frame(frame, others, start_ref, low_ref, high_ref):
    edge = jnp.zeros((PAD, frame.shape[1]), F32)
    for ref in (frame,) + others:
        ref[0:PAD, :] = edge
        ref[PAD + FRAME : PAD + FRAME + PAD, :] = edge
    frame[PAD : PAD + HALO, :] = low_ref[...]
    frame[PAD + HALO : PAD + HALO + ROWS, :] = start_ref[...]
    frame[PAD + HALO + ROWS : PAD + FRAME, :] = high_ref[...]


def low_rows(m):
    first = PAD + HALO - 8 * (m + 1)
    return slice(first, first + 8)


def high_rows(m):
    first = PAD + HALO + ROWS + 8 * m
    return slice(first, first + 8)


def for_halo_blocks(pair, act):
    for m in range(4):
        if m == 0:
            act(m)
        else:
            pl.when(m < 4 - pair)(lambda m=m: act(m))


def add_frame(frame, pair, depth, offset, center, low_ref, high_ref, index):
    frame[PAD + HALO : PAD + HALO + ROWS, :] += center

    def act(m):
        frame[low_rows(m), :] += low_ref[index + (rows8(offset + depth - 8 * (m + 1)),)]
        frame[high_rows(m), :] += high_ref[index + (rows8(offset + 8 * m),)]

    for_halo_blocks(pair, act)


def forward_block(src, dst, first, u, v, mask):
    columns = src.shape[1]
    c = src[first : first + 8, :]
    n = src[first + 1 : first + 9, :]
    s = src[first - 1 : first + 7, :]
    e = pltpu.roll(c, columns - 1, 1)
    w = pltpu.roll(c, 1, 1)
    hu = 0.5 * u
    hv = 0.5 * v
    out = 0.6 * c + (0.1 - hu) * e + (0.1 + hu) * w + (0.1 - hv) * n + (0.1 + hv) * s
    if mask is not None:
        out = out * mask
    dst[first : first + 8, :] = out


def forward_kernel(
    info, start_ref, start_low, start_high, data_ref, data_low, data_high, out_ref, xa, xb
):
    i = pl.program_id(0)
    pair, depth, offset = packed_place(i)
    low_mask = info[1].astype(F32)
    high_mask = info[2].astype(F32)

    @pl.when(i == 0)
    def _():
        start_frame(xa, (xb,), start_ref, start_low, start_high)

    add_frame(xa, pair, depth, offset, data_ref[0, 0], data_low, data_high, (0,))
    for step in range(STEPS):
        src, dst = (xa, xb) if step % 2 == 0 else (xb, xa)
        for b in range(ROWS // 8):
            own = slice(8 * b, 8 * b + 8)
            forward_block(
                src, dst, PAD + HALO + 8 * b, data_ref[0, 1, own, :], data_ref[0, 2, own, :], None
            )

        def act(m):
            low = rows8(offset + depth - 8 * (m + 1))
            high = rows8(offset + 8 * m)
            forward_block(
                src, dst, low_rows(m).start, data_low[1, low, :], data_low[2, low, :], low_mask
            )
            forward_block(
                src, dst, high_rows(m).start, data_high[1, high, :], data_high[2, high, :], high_mask
            )

        for_halo_blocks(pair, act)
    out_ref[0] = xa[PAD + HALO : PAD + HALO + ROWS, :]


def adjoint_block(src, dst, first, u, hv, mask):
    columns = src.shape[1]
    c = src[first : first + 8, :]
    n = src[first + 1 : first + 9, :]
    s = src[first - 1 : first + 7, :]
    hv_n = hv[first + 1 : first + 9, :]
    hv_s = hv[first - 1 : first + 7, :]
    spread = 0.1 * c
    flux = (0.5 * u) * c
    from_east = pltpu.roll(spread + flux, columns - 1, 1)
    from_west = pltpu.roll(spread - flux, 1, 1)
    out = 0.6 * c + from_east + from_west + (0.1 + hv_n) * n + (0.1 - hv_s) * s
    if mask is not None:
        out = out * mask
    dst[first : first + 8, :] = out


def adjoint_kernel(
    info,
    start_ref,
    start_low,
    start_high,
    forcing_ref,
    forcing_low,
    forcing_high,
    data_ref,
    data_low,
    data_high,
    out_ref,
    xa,
    xb,
    hv,
):
    i = pl.program_id(0)
    pair, depth, offset = packed_place(i)
    low_mask = info[1].astype(F32)
    high_mask = info[2].astype(F32)

    @pl.when(i == 0)
    def _():
        start_frame(xa, (xb, hv), start_ref, start_low, start_high)

    add_frame(xa, pair, depth, offset, forcing_ref[0], forcing_low, forcing_high, ())
    hv[PAD + HALO : PAD + HALO + ROWS, :] = 0.5 * data_ref[0, 2]

    def place_wind(m):
        low = rows8(offset + depth - 8 * (m + 1))
        high = rows8(offset + 8 * m)
        hv[low_rows(m), :] = 0.5 * data_low[1, low, :]
        hv[high_rows(m), :] = 0.5 * data_high[1, high, :]

    for_halo_blocks(pair, place_wind)
    for step in range(STEPS):
        src, dst = (xa, xb) if step % 2 == 0 else (xb, xa)
        for b in range(ROWS // 8):
            own = slice(8 * b, 8 * b + 8)
            adjoint_block(src, dst, PAD + HALO + 8 * b, data_ref[0, 1, own, :], hv, None)

        def act(m):
            low = rows8(offset + depth - 8 * (m + 1))
            high = rows8(offset + 8 * m)
            adjoint_block(src, dst, low_rows(m).start, data_low[0, low, :], hv, low_mask)
            adjoint_block(src, dst, high_rows(m).start, data_high[0, high, :], hv, high_mask)

        for_halo_blocks(pair, act)
    out_ref[0] = xa[PAD + HALO : PAD + HALO + ROWS, :]


def forward_pass(info, start, data, data_halo):
    columns = data.shape[3]
    halo = (3, PACKED, columns)
    out = (GROUP, ROWS, columns)
    frame = pltpu.VMEM((FRAME + 2 * PAD, columns), F32)
    return pl.pallas_call(
        forward_kernel,
        grid_spec=pltpu.PrefetchScalarGridSpec(
            num_scalar_prefetch=1,
            grid=(GROUP,),
            in_specs=[
                whole((ROWS, columns)),
                whole((HALO, columns)),
                whole((HALO, columns)),
                pl.BlockSpec((1, 3, ROWS, columns), lambda i, info: (i ^ info[0], 0, 0, 0)),
                whole(halo),
                whole(halo),
            ],
            out_specs=pl.BlockSpec((1, ROWS, columns), lambda i, info: (i, 0, 0)),
            scratch_shapes=[frame] * 2,
        ),
        out_shape=jax.ShapeDtypeStruct(out, F32),
        compiler_params=params(32),
        cost_estimate=cost(32 * 13 * 80 * columns, 8 << 20),
        name="tangent_pass",
    )(info, *start, data, *data_halo)


def adjoint_pass(info, start, forcing, forcing_halo, data, data_halo):
    columns = data.shape[3]
    last = GROUP - 1
    out = (GROUP, ROWS, columns)
    frame = pltpu.VMEM((FRAME + 2 * PAD, columns), F32)
    block = pl.BlockSpec((1, ROWS, columns), lambda i, info: (last - i, 0, 0))
    return pl.pallas_call(
        adjoint_kernel,
        grid_spec=pltpu.PrefetchScalarGridSpec(
            num_scalar_prefetch=1,
            grid=(GROUP,),
            in_specs=[
                whole((ROWS, columns)),
                whole((HALO, columns)),
                whole((HALO, columns)),
                block,
                whole((PACKED, columns)),
                whole((PACKED, columns)),
                pl.BlockSpec(
                    (1, 3, ROWS, columns), lambda i, info: ((last - i) ^ info[0], 0, 0, 0)
                ),
                whole((2, PACKED, columns)),
                whole((2, PACKED, columns)),
            ],
            out_specs=block,
            scratch_shapes=[frame] * 3,
        ),
        out_shape=jax.ShapeDtypeStruct(out, F32),
        compiler_params=params(32),
        cost_estimate=cost(32 * 13 * 80 * columns, 8 << 20),
        name="adjoint_pass",
    )(info, *start, forcing, *forcing_halo, data, *data_halo)


def split(value):
    high = value.astype(BF16)
    return high, (value - high.astype(F32)).astype(BF16)


def product(left, right):
    total = jnp.dot(left[0], right[1], preferred_element_type=F32)
    total = total + jnp.dot(left[1], right[0], preferred_element_type=F32)
    return total + jnp.dot(left[0], right[0], preferred_element_type=F32)


def zonal_kernel(info, adjoint_ref, deviation_ref, table_ref, out_ref, high, low):
    half = out_ref.shape[2]
    for o in range(GROUP):
        scaled = adjoint_ref[o] * deviation_ref[o ^ info[0]]
        high[o * ROWS : (o + 1) * ROWS, :], low[o * ROWS : (o + 1) * ROWS, :] = split(scaled)
    for part in range(2):
        lanes = slice(part * half, (part + 1) * half)
        result = product((high[...], low[...]), (table_ref[0, :, lanes], table_ref[1, :, lanes]))
        for o in range(GROUP):
            out_ref[2 * o + part] = result[o * ROWS : (o + 1) * ROWS, :]


def zonal(info, adjoint, deviation, table):
    vertical, rows, columns = deviation.shape
    out = (2 * vertical, rows, columns // 2)
    return pl.pallas_call(
        zonal_kernel,
        grid_spec=pltpu.PrefetchScalarGridSpec(
            num_scalar_prefetch=1,
            grid=(1,),
            in_specs=[whole(adjoint.shape), whole(deviation.shape), whole(table.shape)],
            out_specs=whole(out),
            scratch_shapes=[pltpu.VMEM((vertical * rows, columns), BF16)] * 2,
        ),
        out_shape=jax.ShapeDtypeStruct(out, F32),
        compiler_params=params(32),
        cost_estimate=cost(6 * vertical * rows * columns * columns, 6 << 20),
        name="zonal_forward",
    )(info, adjoint, deviation, table)


def meridional_kernel(bands_ref, spectrum_ref, table_ref, back_ref, out_ref):
    merid = product((table_ref[0], table_ref[1]), split(bands_ref[...])) * spectrum_ref[...]
    out_ref[...] = product((back_ref[0], back_ref[1]), split(merid))


def meridional(bands, spectrum, table, back):
    return pl.pallas_call(
        meridional_kernel,
        grid=(1,),
        in_specs=[whole(x.shape) for x in (bands, spectrum, table, back)],
        out_specs=whole(bands.shape),
        out_shape=jax.ShapeDtypeStruct(bands.shape, F32),
        compiler_params=params(40),
        cost_estimate=cost(12 * bands.shape[0] * bands.size, 9 << 20),
        name="meridional",
    )(bands, spectrum, table, back)


def zonal_back_kernel(info, bands_ref, deviation_ref, increments_ref, table_ref, out_ref, high, low):
    half = bands_ref.shape[2]
    for o in range(GROUP):
        for part in range(2):
            rows = slice(o * ROWS, (o + 1) * ROWS)
            lanes = slice(part * half, (part + 1) * half)
            high[rows, lanes], low[rows, lanes] = split(bands_ref[2 * o + part])
    result = product((high[...], low[...]), (table_ref[0], table_ref[1]))
    for o in range(GROUP):
        v = o ^ info[0]
        rows = slice(o * ROWS, (o + 1) * ROWS)
        out_ref[v] = increments_ref[v] + deviation_ref[v] * result[rows, :]


def zonal_back(info, bands, deviation, increments, table):
    vertical, rows, columns = deviation.shape
    return pl.pallas_call(
        zonal_back_kernel,
        grid_spec=pltpu.PrefetchScalarGridSpec(
            num_scalar_prefetch=1,
            grid=(1,),
            in_specs=[whole(x.shape) for x in (bands, deviation, increments, table)],
            out_specs=whole(deviation.shape),
            scratch_shapes=[pltpu.VMEM((vertical * rows, columns), BF16)] * 2,
        ),
        out_shape=jax.ShapeDtypeStruct(deviation.shape, F32),
        compiler_params=params(40),
        cost_estimate=cost(6 * vertical * rows * columns * columns, 7 << 20),
        name="zonal_back",
    )(info, bands, deviation, increments, table)


def trade(pieces, count):
    return [pieces[0]] + [
        lax.ppermute(pieces[o], "tm", [(i, i ^ o) for i in range(count)]) for o in range(1, GROUP)
    ]


def slab_rims(up, down, shift):
    tm, slabs = lax.axis_size("tm"), lax.axis_size("slab")
    at = lambda t, s: t * slabs + s
    pairs = [(t, t + shift) for t in range(tm) if 0 <= t + shift < tm]
    low = [(at(t, s), at(u, s + 1)) for t, u in pairs for s in range(slabs - 1)]
    high = [(at(t, s + 1), at(u, s)) for t, u in pairs for s in range(slabs - 1)]
    axes = ("tm", "slab")
    return lax.ppermute(up, axes, low), lax.ppermute(down, axes, high)


def next_group(state, shift):
    tm = lax.axis_size("tm")
    low, high = slab_rims(state[ROWS - HALO :], state[:HALO], shift)
    pairs = [(t, t + shift) for t in range(tm) if 0 <= t + shift < tm]
    return lax.ppermute(state, "tm", pairs), low, high


def body(increments, courant, deviation, spectrum, observed_cells, innovation, error_weights):
    tm, slabs = lax.axis_size("tm"), lax.axis_size("slab")
    place = lax.axis_index("tm") % GROUP
    slab = lax.axis_index("slab")
    info = jnp.stack([place, slab > 0, slab < slabs - 1]).astype(jnp.int32)
    state = increments[0].transpose(1, 0, 2)
    vertical, row_count, columns = state.shape
    winds = courant[0].transpose(1, 0, 2)
    pick = lambda array, o: lax.dynamic_index_in_dim(array, place ^ o, 0, keepdims=False)

    pieces = [
        jnp.concatenate([pick(state, o)[None], winds], axis=0) for o in range(GROUP)
    ]
    data = jnp.stack(trade(pieces, tm))
    up, down = pack(info, data, 0, False)
    data_halo = slab_rims(up, down, 0)

    maps = scatter(observed_cells[0], error_weights[0], innovation[0], vertical, columns)
    maps = jnp.stack(trade([pick(maps, o) for o in range(GROUP)], tm))

    zero = jnp.zeros((row_count, columns), F32)
    rim = jnp.zeros((HALO, columns), F32)
    ends = forward_pass(info, (zero, rim, rim), data, data_halo)
    ends = forward_pass(info, next_group(ends[GROUP - 1], GROUP), data, data_halo)

    up, down = pack(info, data, 1, True)
    wind_halo = slab_rims(up, down, 0)
    forcing, up, down = forcing_of(info, maps, ends)
    forcing_halo = slab_rims(up, down, 0)
    starts = adjoint_pass(info, (zero, rim, rim), forcing, forcing_halo, data, wind_halo)
    starts = adjoint_pass(
        info, next_group(starts[0], -GROUP), forcing, forcing_halo, data, wind_halo
    )
    adjoint = jnp.stack(trade([pick(starts, o) for o in range(GROUP)], tm))

    zonal_table = jnp.asarray(split_table(hartley_table(columns)))
    cosine = cosine_table(slabs * row_count)
    merid_table = jnp.asarray(split_table(cosine))
    merid_back = jnp.asarray(split_table(cosine.T))
    deviation = deviation.transpose(1, 0, 2)
    waves = lax.all_gather(spectrum.T, "slab", tiled=True)
    half = columns // 2
    waves = lax.dynamic_slice_in_dim(waves, (slab % 2) * half, half, 0).T

    bands = zonal(info, adjoint, deviation, zonal_table)
    bands = lax.all_to_all(bands, "slab", 0, 0, tiled=True)
    bands = meridional(bands.reshape(slabs * row_count, half), waves, merid_table, merid_back)
    bands = lax.all_to_all(bands.reshape(slabs, row_count, half), "slab", 0, 0, tiled=True)
    gradient = zonal_back(info, bands, deviation, state, zonal_table)
    return gradient.transpose(1, 0, 2)[None]


def solution(mesh):
    in_specs = (
        P("tm", "slab", None, None),
        P("tm", "slab", None, None),
        P("slab", None, None),
        P(None, "slab"),
        P("tm", "slab"),
        P("tm", "slab"),
        P("tm", "slab"),
    )
    out_specs = P("tm", "slab", None, None)
    return jax.shard_map(body, mesh=mesh, in_specs=in_specs, out_specs=out_specs, check_vma=False)
```

```python
import functools
import math

import jax
import jax.numpy as jnp
import numpy as np
from jax import lax
from jax.experimental import pallas as pl
from jax.experimental.pallas import tpu as pltpu
from jax.sharding import PartitionSpec as P

STEPS = 4
GROUP = 8
HALO = 32
ROWS = 48
FRAME = ROWS + 2 * HALO
PAD = 8
PACKED = 160
FAR_FIRST = (6, 2, 7, 5, 3, 1, 4)
Y_FIRST = (6, 7, 5, 4, 2, 3, 1)
F32 = jnp.float32
BF16 = jnp.bfloat16


def split_table(table):
    high = table.astype(jnp.bfloat16)
    low = (table - high.astype(np.float64)).astype(jnp.bfloat16)
    return np.stack([high, low])


def hartley_table(length):
    index = np.arange(length)
    angle = (index[:, None] * index[None, :] % length) * (2.0 * math.pi / length)
    return (np.cos(angle) + np.sin(angle)) / math.sqrt(length)


def cosine_table(length):
    index = np.arange(length)
    angle = ((2 * index[None, :] + 1) * index[:, None] % (4 * length)) * (math.pi / (2 * length))
    scales = np.where(index == 0, math.sqrt(1.0 / length), math.sqrt(2.0 / length))
    return scales[:, None] * np.cos(angle)


def params(megabytes, grid=True):
    return pltpu.CompilerParams(
        vmem_limit_bytes=megabytes * 1024 * 1024,
        dimension_semantics=("arbitrary",) if grid else None,
    )


def cost(flops, size):
    return pl.CostEstimate(flops=flops, bytes_accessed=size, transcendentals=0)


def whole(shape):
    return pl.BlockSpec(shape, lambda *_: (0,) * len(shape))


def packed_place(i):
    pair = lax.shift_right_logical(i, 1)
    depth = 32 - 8 * pair
    offset = 64 * pair - 8 * pair * (pair - 1) + (i & 1) * depth
    return pair, depth, offset


def rows8(start):
    return pl.ds(pl.multiple_of(start, 8), 8)


def scatter_kernel(row_ref, col_ref, w_ref, z_ref, *rest):
    before, (out_ref, acc) = rest[:-2], rest[-2:]
    step = pl.program_id(0)
    rows, cols = acc.shape[1], acc.shape[2]
    count = row_ref.shape[-1]

    @pl.when(step == 0)
    def _():
        if not before:
            acc[...] = jnp.zeros_like(acc)
        else:
            for v in range(rows // ROWS):
                for which in range(2):
                    acc[which, v * ROWS : (v + 1) * ROWS, :] = before[0][v, which]

    row_iota = lax.broadcasted_iota(jnp.int32, (rows, count), 0)
    col_iota = lax.broadcasted_iota(jnp.int32, (cols, count), 0)
    at_row = jnp.where(row_iota == row_ref[0], 1.0, 0.0).astype(BF16)
    at_col = jnp.where(col_iota == col_ref[0], 1.0, 0.0).astype(BF16)
    for which, ref in enumerate((w_ref, z_ref)):
        value = ref[0]
        high = value.astype(BF16)
        low = (value - high.astype(F32)).astype(BF16)
        for part in (high, low):
            acc[which] += lax.dot_general(
                at_row * part, at_col, (((1,), (1,)), ((), ())), preferred_element_type=F32
            )

    @pl.when(step == pl.num_programs(0) - 1)
    def _():
        for v in range(rows // ROWS):
            for which in range(2):
                out_ref[v, which] = acc[which, v * ROWS : (v + 1) * ROWS, :]


def scatter(cells, weights, innovation, vertical, columns):
    count = cells.shape[0]
    chunk = 1024
    line = cells // columns
    col = cells - line * columns
    row = (line % vertical) * ROWS + line // vertical
    shape = (count // chunk, 1, chunk)
    operands = [x.reshape(shape) for x in (row, col, weights, weights * innovation)]
    halves = count // chunk // 2
    out = (vertical, 2, ROWS, columns)
    maps = []
    for part in range(2):
        spec = pl.BlockSpec((1, 1, chunk), lambda i, part=part: (i + part * halves, 0, 0))
        maps = [
            pl.pallas_call(
                scatter_kernel,
                grid=(halves,),
                in_specs=[spec] * 4 + [whole(out)] * part,
                out_specs=whole(out),
                out_shape=jax.ShapeDtypeStruct(out, F32),
                scratch_shapes=[pltpu.VMEM((2, vertical * ROWS, columns), F32)],
                compiler_params=params(40),
                cost_estimate=cost(2 * 4 * count // 2 * vertical * ROWS * columns, 4 << 20),
                name=f"observation_maps_{part}",
            )(*operands, *maps)
        ]
    return maps[0]


def pack_kernel(skip, reverse, info, data_ref, up_ref, down_ref):
    k = pl.program_id(0)
    pair, depth, offset = packed_place(GROUP - 1 - k if reverse else k)
    for m in range(4):

        @pl.when(m < 4 - pair)
        def _():
            up_ref[:, rows8(offset + depth - 8 * (m + 1)), :] = data_ref[
                0, skip:, ROWS - 8 * (m + 1) : ROWS - 8 * m, :
            ]
            down_ref[:, rows8(offset + 8 * m), :] = data_ref[0, skip:, 8 * m : 8 * m + 8, :]


def pack(info, data, skip, reverse):
    parts, columns = data.shape[1], data.shape[3]
    out = (parts - skip, PACKED, columns)
    return pl.pallas_call(
        functools.partial(pack_kernel, skip, reverse),
        grid_spec=pltpu.PrefetchScalarGridSpec(
            num_scalar_prefetch=1,
            grid=(GROUP,),
            in_specs=[
                pl.BlockSpec((1, parts, ROWS, columns), lambda k, info: (k ^ info[0], 0, 0, 0))
            ],
            out_specs=[whole(out), whole(out)],
        ),
        out_shape=[jax.ShapeDtypeStruct(out, F32)] * 2,
        compiler_params=params(24),
        cost_estimate=cost(0, 6 << 20),
        name="pack_adjoint_halo" if reverse else "pack_halo",
    )(info, data)


def forcing_kernel(info, maps_ref, end_ref, out_ref, up_ref, down_ref):
    k = pl.program_id(0)
    pair, depth, offset = packed_place(GROUP - 1 - k)
    forcing = maps_ref[0, 0] * end_ref[0] - maps_ref[0, 1]
    out_ref[0] = forcing
    for m in range(4):

        @pl.when(m < 4 - pair)
        def _():
            up_ref[rows8(offset + depth - 8 * (m + 1)), :] = forcing[
                ROWS - 8 * (m + 1) : ROWS - 8 * m, :
            ]
            down_ref[rows8(offset + 8 * m), :] = forcing[8 * m : 8 * m + 8, :]


def forcing_of(info, maps, ends):
    columns = ends.shape[2]
    out = (PACKED, columns)
    block = pl.BlockSpec((1, ROWS, columns), lambda k, info: (k, 0, 0))
    return pl.pallas_call(
        forcing_kernel,
        grid_spec=pltpu.PrefetchScalarGridSpec(
            num_scalar_prefetch=1,
            grid=(GROUP,),
            in_specs=[
                pl.BlockSpec((1, 2, ROWS, columns), lambda k, info: (k ^ info[0], 0, 0, 0)),
                block,
            ],
            out_specs=[block, whole(out), whole(out)],
        ),
        out_shape=[jax.ShapeDtypeStruct(ends.shape, F32)]
        + [jax.ShapeDtypeStruct(out, F32)] * 2,
        compiler_params=params(16),
        cost_estimate=cost(1 << 20, 6 << 20),
        name="forcing",
    )(info, maps, ends)


def start_frame(frame, others, start_ref, low_ref, high_ref):
    edge = jnp.zeros((PAD, frame.shape[1]), F32)
    for ref in (frame,) + others:
        ref[0:PAD, :] = edge
        ref[PAD + FRAME : PAD + FRAME + PAD, :] = edge
    frame[PAD : PAD + HALO, :] = low_ref[...]
    frame[PAD + HALO : PAD + HALO + ROWS, :] = start_ref[...]
    frame[PAD + HALO + ROWS : PAD + FRAME, :] = high_ref[...]


def low_rows(m):
    first = PAD + HALO - 8 * (m + 1)
    return slice(first, first + 8)


def high_rows(m):
    first = PAD + HALO + ROWS + 8 * m
    return slice(first, first + 8)


def for_halo_blocks(pair, act):
    for m in range(4):
        if m == 0:
            act(m)
        else:
            pl.when(m < 4 - pair)(lambda m=m: act(m))


def add_frame(frame, pair, depth, offset, center, low_ref, high_ref, index):
    frame[PAD + HALO : PAD + HALO + ROWS, :] += center

    def act(m):
        frame[low_rows(m), :] += low_ref[index + (rows8(offset + depth - 8 * (m + 1)),)]
        frame[high_rows(m), :] += high_ref[index + (rows8(offset + 8 * m),)]

    for_halo_blocks(pair, act)


def forward_block(src, dst, first, u, v, mask):
    columns = src.shape[1]
    c = src[first : first + 8, :]
    n = src[first + 1 : first + 9, :]
    s = src[first - 1 : first + 7, :]
    e = pltpu.roll(c, columns - 1, 1)
    w = pltpu.roll(c, 1, 1)
    hu = 0.5 * u
    hv = 0.5 * v
    out = 0.6 * c + (0.1 - hu) * e + (0.1 + hu) * w + (0.1 - hv) * n + (0.1 + hv) * s
    if mask is not None:
        out = out * mask
    dst[first : first + 8, :] = out


def forward_kernel(
    info, start_ref, start_low, start_high, data_ref, data_low, data_high, out_ref, xa, xb
):
    i = pl.program_id(0)
    pair, depth, offset = packed_place(i)
    low_mask = info[1].astype(F32)
    high_mask = info[2].astype(F32)

    @pl.when(i == 0)
    def _():
        start_frame(xa, (xb,), start_ref, start_low, start_high)

    add_frame(xa, pair, depth, offset, data_ref[0, 0], data_low, data_high, (0,))
    for step in range(STEPS):
        src, dst = (xa, xb) if step % 2 == 0 else (xb, xa)
        for b in range(ROWS // 8):
            own = slice(8 * b, 8 * b + 8)
            forward_block(
                src, dst, PAD + HALO + 8 * b, data_ref[0, 1, own, :], data_ref[0, 2, own, :], None
            )

        def act(m):
            low = rows8(offset + depth - 8 * (m + 1))
            high = rows8(offset + 8 * m)
            forward_block(
                src, dst, low_rows(m).start, data_low[1, low, :], data_low[2, low, :], low_mask
            )
            forward_block(
                src, dst, high_rows(m).start, data_high[1, high, :], data_high[2, high, :], high_mask
            )

        for_halo_blocks(pair, act)
    out_ref[0] = xa[PAD + HALO : PAD + HALO + ROWS, :]


def adjoint_block(src, dst, first, u, hv, mask):
    columns = src.shape[1]
    c = src[first : first + 8, :]
    n = src[first + 1 : first + 9, :]
    s = src[first - 1 : first + 7, :]
    hv_n = hv[first + 1 : first + 9, :]
    hv_s = hv[first - 1 : first + 7, :]
    spread = 0.1 * c
    flux = (0.5 * u) * c
    from_east = pltpu.roll(spread + flux, columns - 1, 1)
    from_west = pltpu.roll(spread - flux, 1, 1)
    out = 0.6 * c + from_east + from_west + (0.1 + hv_n) * n + (0.1 - hv_s) * s
    if mask is not None:
        out = out * mask
    dst[first : first + 8, :] = out


def adjoint_kernel(
    info,
    start_ref,
    start_low,
    start_high,
    forcing_ref,
    forcing_low,
    forcing_high,
    data_ref,
    data_low,
    data_high,
    out_ref,
    xa,
    xb,
    hv,
):
    i = pl.program_id(0)
    pair, depth, offset = packed_place(i)
    low_mask = info[1].astype(F32)
    high_mask = info[2].astype(F32)

    @pl.when(i == 0)
    def _():
        start_frame(xa, (xb, hv), start_ref, start_low, start_high)

    add_frame(xa, pair, depth, offset, forcing_ref[0], forcing_low, forcing_high, ())
    hv[PAD + HALO : PAD + HALO + ROWS, :] = 0.5 * data_ref[0, 2]

    def place_wind(m):
        low = rows8(offset + depth - 8 * (m + 1))
        high = rows8(offset + 8 * m)
        hv[low_rows(m), :] = 0.5 * data_low[1, low, :]
        hv[high_rows(m), :] = 0.5 * data_high[1, high, :]

    for_halo_blocks(pair, place_wind)
    for step in range(STEPS):
        src, dst = (xa, xb) if step % 2 == 0 else (xb, xa)
        for b in range(ROWS // 8):
            own = slice(8 * b, 8 * b + 8)
            adjoint_block(src, dst, PAD + HALO + 8 * b, data_ref[0, 1, own, :], hv, None)

        def act(m):
            low = rows8(offset + depth - 8 * (m + 1))
            high = rows8(offset + 8 * m)
            adjoint_block(src, dst, low_rows(m).start, data_low[0, low, :], hv, low_mask)
            adjoint_block(src, dst, high_rows(m).start, data_high[0, high, :], hv, high_mask)

        for_halo_blocks(pair, act)
    out_ref[0] = xa[PAD + HALO : PAD + HALO + ROWS, :]


def forward_pass(info, start, data, data_halo):
    columns = data.shape[3]
    halo = (3, PACKED, columns)
    out = (GROUP, ROWS, columns)
    frame = pltpu.VMEM((FRAME + 2 * PAD, columns), F32)
    return pl.pallas_call(
        forward_kernel,
        grid_spec=pltpu.PrefetchScalarGridSpec(
            num_scalar_prefetch=1,
            grid=(GROUP,),
            in_specs=[
                whole((ROWS, columns)),
                whole((HALO, columns)),
                whole((HALO, columns)),
                pl.BlockSpec((1, 3, ROWS, columns), lambda i, info: (i ^ info[0], 0, 0, 0)),
                whole(halo),
                whole(halo),
            ],
            out_specs=pl.BlockSpec((1, ROWS, columns), lambda i, info: (i, 0, 0)),
            scratch_shapes=[frame] * 2,
        ),
        out_shape=jax.ShapeDtypeStruct(out, F32),
        compiler_params=params(32),
        cost_estimate=cost(32 * 13 * 80 * columns, 8 << 20),
        name="tangent_pass",
    )(info, *start, data, *data_halo)


def adjoint_pass(info, start, forcing, forcing_halo, data, data_halo):
    columns = data.shape[3]
    last = GROUP - 1
    out = (GROUP, ROWS, columns)
    frame = pltpu.VMEM((FRAME + 2 * PAD, columns), F32)
    block = pl.BlockSpec((1, ROWS, columns), lambda i, info: (last - i, 0, 0))
    return pl.pallas_call(
        adjoint_kernel,
        grid_spec=pltpu.PrefetchScalarGridSpec(
            num_scalar_prefetch=1,
            grid=(GROUP,),
            in_specs=[
                whole((ROWS, columns)),
                whole((HALO, columns)),
                whole((HALO, columns)),
                block,
                whole((PACKED, columns)),
                whole((PACKED, columns)),
                pl.BlockSpec(
                    (1, 3, ROWS, columns), lambda i, info: ((last - i) ^ info[0], 0, 0, 0)
                ),
                whole((2, PACKED, columns)),
                whole((2, PACKED, columns)),
            ],
            out_specs=block,
            scratch_shapes=[frame] * 3,
        ),
        out_shape=jax.ShapeDtypeStruct(out, F32),
        compiler_params=params(32),
        cost_estimate=cost(32 * 13 * 80 * columns, 8 << 20),
        name="adjoint_pass",
    )(info, *start, forcing, *forcing_halo, data, *data_halo)


def split(value):
    high = value.astype(BF16)
    return high, (value - high.astype(F32)).astype(BF16)


def product(left, right):
    total = jnp.dot(left[0], right[1], preferred_element_type=F32)
    total = total + jnp.dot(left[1], right[0], preferred_element_type=F32)
    return total + jnp.dot(left[0], right[0], preferred_element_type=F32)


def zonal_kernel(info, adjoint_ref, deviation_ref, table_ref, out_ref, high, low):
    half = out_ref.shape[2]
    for o in range(GROUP):
        scaled = adjoint_ref[o] * deviation_ref[o ^ info[0]]
        high[o * ROWS : (o + 1) * ROWS, :], low[o * ROWS : (o + 1) * ROWS, :] = split(scaled)
    for part in range(2):
        lanes = slice(part * half, (part + 1) * half)
        result = product((high[...], low[...]), (table_ref[0, :, lanes], table_ref[1, :, lanes]))
        for o in range(GROUP):
            out_ref[2 * o + part] = result[o * ROWS : (o + 1) * ROWS, :]


def zonal(info, adjoint, deviation, table):
    vertical, rows, columns = deviation.shape
    out = (2 * vertical, rows, columns // 2)
    return pl.pallas_call(
        zonal_kernel,
        grid_spec=pltpu.PrefetchScalarGridSpec(
            num_scalar_prefetch=1,
            grid=(1,),
            in_specs=[whole(adjoint.shape), whole(deviation.shape), whole(table.shape)],
            out_specs=whole(out),
            scratch_shapes=[pltpu.VMEM((vertical * rows, columns), BF16)] * 2,
        ),
        out_shape=jax.ShapeDtypeStruct(out, F32),
        compiler_params=params(32),
        cost_estimate=cost(6 * vertical * rows * columns * columns, 6 << 20),
        name="zonal_forward",
    )(info, adjoint, deviation, table)


def meridional_kernel(bands_ref, spectrum_ref, table_ref, back_ref, out_ref):
    merid = product((table_ref[0], table_ref[1]), split(bands_ref[...])) * spectrum_ref[...]
    out_ref[...] = product((back_ref[0], back_ref[1]), split(merid))


def meridional(bands, spectrum, table, back):
    return pl.pallas_call(
        meridional_kernel,
        grid=(1,),
        in_specs=[whole(x.shape) for x in (bands, spectrum, table, back)],
        out_specs=whole(bands.shape),
        out_shape=jax.ShapeDtypeStruct(bands.shape, F32),
        compiler_params=params(40),
        cost_estimate=cost(12 * bands.shape[0] * bands.size, 9 << 20),
        name="meridional",
    )(bands, spectrum, table, back)


def zonal_back_kernel(info, bands_ref, deviation_ref, increments_ref, table_ref, out_ref, high, low):
    half = bands_ref.shape[2]
    for o in range(GROUP):
        for part in range(2):
            rows = slice(o * ROWS, (o + 1) * ROWS)
            lanes = slice(part * half, (part + 1) * half)
            high[rows, lanes], low[rows, lanes] = split(bands_ref[2 * o + part])
    result = product((high[...], low[...]), (table_ref[0], table_ref[1]))
    for o in range(GROUP):
        v = o ^ info[0]
        rows = slice(o * ROWS, (o + 1) * ROWS)
        out_ref[v] = increments_ref[v] + deviation_ref[v] * result[rows, :]


def zonal_back(info, bands, deviation, increments, table):
    vertical, rows, columns = deviation.shape
    return pl.pallas_call(
        zonal_back_kernel,
        grid_spec=pltpu.PrefetchScalarGridSpec(
            num_scalar_prefetch=1,
            grid=(1,),
            in_specs=[whole(x.shape) for x in (bands, deviation, increments, table)],
            out_specs=whole(deviation.shape),
            scratch_shapes=[pltpu.VMEM((vertical * rows, columns), BF16)] * 2,
        ),
        out_shape=jax.ShapeDtypeStruct(deviation.shape, F32),
        compiler_params=params(40),
        cost_estimate=cost(6 * vertical * rows * columns * columns, 7 << 20),
        name="zonal_back",
    )(info, bands, deviation, increments, table)


def trade(pieces, count):
    swap = lambda piece, o: lax.ppermute(piece, "tm", [(i, i ^ o) for i in range(count)])
    return {o: swap(piece, o) if o else piece for o, piece in pieces.items()}


def in_order(pieces):
    return jnp.stack([pieces[o] for o in range(GROUP)])


def slab_rims(up, down, shift):
    tm, slabs = lax.axis_size("tm"), lax.axis_size("slab")
    at = lambda t, s: t * slabs + s
    pairs = [(t, t + shift) for t in range(tm) if 0 <= t + shift < tm]
    low = [(at(t, s), at(u, s + 1)) for t, u in pairs for s in range(slabs - 1)]
    high = [(at(t, s + 1), at(u, s)) for t, u in pairs for s in range(slabs - 1)]
    axes = ("tm", "slab")
    return lax.ppermute(up, axes, low), lax.ppermute(down, axes, high)


def next_group(state, shift):
    tm = lax.axis_size("tm")
    pairs = [(t, t + shift) for t in range(tm) if 0 <= t + shift < tm]
    middle = lax.ppermute(state, "tm", pairs)
    low, high = slab_rims(state[ROWS - HALO :], state[:HALO], shift)
    return middle, low, high


def body(increments, courant, deviation, spectrum, observed_cells, innovation, error_weights):
    tm, slabs = lax.axis_size("tm"), lax.axis_size("slab")
    place = lax.axis_index("tm") % GROUP
    slab = lax.axis_index("slab")
    info = jnp.stack([place, slab > 0, slab < slabs - 1]).astype(jnp.int32)
    state = increments[0].transpose(1, 0, 2)
    vertical, row_count, columns = state.shape
    winds = courant[0].transpose(1, 0, 2)
    pick = lambda array, o: lax.dynamic_index_in_dim(array, place ^ o, 0, keepdims=False)

    pieces = {
        o: jnp.concatenate([pick(state, o)[None], winds], axis=0) for o in (0,) + FAR_FIRST
    }
    data = in_order(trade(pieces, tm))
    parity = [list(range(c, slabs, 2)) for c in range(2)]
    waves = lax.all_gather(spectrum.T, "slab", axis_index_groups=parity, tiled=True)
    maps = scatter(observed_cells[0], error_weights[0], innovation[0], vertical, columns)
    data, waves, maps = lax.optimization_barrier((data, waves, maps))
    up, down = pack(info, data, 0, False)
    maps, up, down = lax.optimization_barrier((maps, up, down))
    data_halo = slab_rims(up, down, 0)
    moved = trade({o: pick(maps, o) for o in (0,) + Y_FIRST}, tm)

    zero = jnp.zeros((row_count, columns), F32)
    rim = jnp.zeros((HALO, columns), F32)
    ends = forward_pass(info, (zero, rim, rim), data, data_halo)
    start = next_group(ends[GROUP - 1], GROUP)
    late, start = lax.optimization_barrier((data, start))
    up, down = pack(info, late, 1, True)
    wind_halo = slab_rims(up, down, 0)
    ends = forward_pass(info, start, data, data_halo)

    forcing, up, down = forcing_of(info, in_order(moved), ends)
    forcing_halo = slab_rims(up, down, 0)
    starts = adjoint_pass(info, (zero, rim, rim), forcing, forcing_halo, data, wind_halo)
    starts = adjoint_pass(
        info, next_group(starts[0], -GROUP), forcing, forcing_halo, data, wind_halo
    )
    adjoint = in_order(trade({o: pick(starts, o) for o in (0,) + FAR_FIRST}, tm))

    half = columns // 2
    order = np.arange(columns).reshape(slabs // 2, 2, -1).transpose(1, 0, 2).reshape(-1)
    zonal_table = hartley_table(columns)[:, order]
    zonal_table, zonal_inverse = (
        jnp.asarray(split_table(table)) for table in (zonal_table, zonal_table.T)
    )
    cosine = cosine_table(slabs * row_count)
    merid_table = jnp.asarray(split_table(cosine))
    merid_back = jnp.asarray(split_table(cosine.T))
    deviation = deviation.transpose(1, 0, 2)
    waves = waves.T

    bands = zonal(info, adjoint, deviation, zonal_table)
    bands = lax.all_to_all(bands, "slab", 0, 0, tiled=True)
    bands = meridional(bands.reshape(slabs * row_count, half), waves, merid_table, merid_back)
    bands = lax.all_to_all(bands.reshape(slabs, row_count, half), "slab", 0, 0, tiled=True)
    gradient = zonal_back(info, bands, deviation, state, zonal_inverse)
    return gradient.transpose(1, 0, 2)[None]


def solution(mesh):
    in_specs = (
        P("tm", "slab", None, None),
        P("tm", "slab", None, None),
        P("slab", None, None),
        P(None, "slab"),
        P("tm", "slab"),
        P("tm", "slab"),
        P("tm", "slab"),
    )
    out_specs = P("tm", "slab", None, None)
    return jax.shard_map(body, mesh=mesh, in_specs=in_specs, out_specs=out_specs, check_vma=False)
```

```python
import functools
import math

import jax
import jax.numpy as jnp
import numpy as np
from jax import lax
from jax.experimental import pallas as pl
from jax.experimental.pallas import tpu as pltpu
from jax.sharding import PartitionSpec as P

STEPS = 4
GROUP = 8
HALO = 32
ROWS = 48
FRAME = ROWS + 2 * HALO
PAD = 8
PACKED = 160
FAR_FIRST = (6, 2, 7, 5, 3, 1, 4)
Y_FIRST = (6, 7, 5, 4, 2, 3, 1)
F32 = jnp.float32
BF16 = jnp.bfloat16


def split_table(table):
    high = table.astype(jnp.bfloat16)
    low = (table - high.astype(np.float64)).astype(jnp.bfloat16)
    return np.stack([high, low])


def hartley_table(length):
    index = np.arange(length)
    angle = (index[:, None] * index[None, :] % length) * (2.0 * math.pi / length)
    return (np.cos(angle) + np.sin(angle)) / math.sqrt(length)


def cosine_table(length):
    index = np.arange(length)
    angle = ((2 * index[None, :] + 1) * index[:, None] % (4 * length)) * (math.pi / (2 * length))
    scales = np.where(index == 0, math.sqrt(1.0 / length), math.sqrt(2.0 / length))
    return scales[:, None] * np.cos(angle)


def params(megabytes, grid=True):
    return pltpu.CompilerParams(
        vmem_limit_bytes=megabytes * 1024 * 1024,
        dimension_semantics=("arbitrary",) if grid else None,
    )


def in_place(count):
    return [pl.BlockSpec(memory_space=pltpu.SMEM)] + [pl.BlockSpec(memory_space=pltpu.VMEM)] * count


def cost(flops, size):
    return pl.CostEstimate(flops=flops, bytes_accessed=size, transcendentals=0)


def whole(shape):
    return pl.BlockSpec(shape, lambda *_: (0,) * len(shape))


def packed_place(i):
    pair = lax.shift_right_logical(i, 1)
    depth = 32 - 8 * pair
    offset = 64 * pair - 8 * pair * (pair - 1) + (i & 1) * depth
    return pair, depth, offset


def rows8(start):
    return pl.ds(pl.multiple_of(start, 8), 8)


def scatter_kernel(row_ref, col_ref, w_ref, z_ref, *rest):
    before, (out_ref, acc) = rest[:-2], rest[-2:]
    step = pl.program_id(0)
    rows, cols = acc.shape[1], acc.shape[2]
    count = row_ref.shape[-1]

    @pl.when(step == 0)
    def _():
        if not before:
            acc[...] = jnp.zeros_like(acc)
        else:
            for v in range(rows // ROWS):
                for which in range(2):
                    acc[which, v * ROWS : (v + 1) * ROWS, :] = before[0][v, which]

    row_iota = lax.broadcasted_iota(jnp.int32, (rows, count), 0)
    col_iota = lax.broadcasted_iota(jnp.int32, (cols, count), 0)
    at_row = jnp.where(row_iota == row_ref[0], 1.0, 0.0).astype(BF16)
    at_col = jnp.where(col_iota == col_ref[0], 1.0, 0.0).astype(BF16)
    for which, ref in enumerate((w_ref, z_ref)):
        value = ref[0]
        high = value.astype(BF16)
        low = (value - high.astype(F32)).astype(BF16)
        for part in (high, low):
            acc[which] += lax.dot_general(
                at_row * part, at_col, (((1,), (1,)), ((), ())), preferred_element_type=F32
            )

    @pl.when(step == pl.num_programs(0) - 1)
    def _():
        for v in range(rows // ROWS):
            for which in range(2):
                out_ref[v, which] = acc[which, v * ROWS : (v + 1) * ROWS, :]


def scatter(cells, weights, innovation, vertical, columns):
    count = cells.shape[0]
    chunk = 1024
    line = cells // columns
    col = cells - line * columns
    row = (line % vertical) * ROWS + line // vertical
    shape = (count // chunk, 1, chunk)
    operands = [x.reshape(shape) for x in (row, col, weights, weights * innovation)]
    halves = count // chunk // 2
    out = (vertical, 2, ROWS, columns)
    maps = []
    for part in range(2):
        spec = pl.BlockSpec((1, 1, chunk), lambda i, part=part: (i + part * halves, 0, 0))
        maps = [
            pl.pallas_call(
                scatter_kernel,
                grid=(halves,),
                in_specs=[spec] * 4 + [whole(out)] * part,
                out_specs=whole(out),
                out_shape=jax.ShapeDtypeStruct(out, F32),
                scratch_shapes=[pltpu.VMEM((2, vertical * ROWS, columns), F32)],
                compiler_params=params(40),
                cost_estimate=cost(2 * 4 * count // 2 * vertical * ROWS * columns, 4 << 20),
                name=f"observation_maps_{part}",
            )(*operands, *maps)
        ]
    return maps[0]


def pack_kernel(skip, reverse, info, data_ref, up_ref, down_ref):
    k = pl.program_id(0)
    pair, depth, offset = packed_place(GROUP - 1 - k if reverse else k)
    for m in range(4):

        @pl.when(m < 4 - pair)
        def _():
            up_ref[:, rows8(offset + depth - 8 * (m + 1)), :] = data_ref[
                0, skip:, ROWS - 8 * (m + 1) : ROWS - 8 * m, :
            ]
            down_ref[:, rows8(offset + 8 * m), :] = data_ref[0, skip:, 8 * m : 8 * m + 8, :]


def pack(info, data, skip, reverse):
    parts, columns = data.shape[1], data.shape[3]
    out = (parts - skip, PACKED, columns)
    return pl.pallas_call(
        functools.partial(pack_kernel, skip, reverse),
        grid_spec=pltpu.PrefetchScalarGridSpec(
            num_scalar_prefetch=1,
            grid=(GROUP,),
            in_specs=[
                pl.BlockSpec((1, parts, ROWS, columns), lambda k, info: (k ^ info[0], 0, 0, 0))
            ],
            out_specs=[whole(out), whole(out)],
        ),
        out_shape=[jax.ShapeDtypeStruct(out, F32)] * 2,
        compiler_params=params(24),
        cost_estimate=cost(0, 6 << 20),
        name="pack_adjoint_halo" if reverse else "pack_halo",
    )(info, data)


def forcing_kernel(info, maps_ref, end_ref, out_ref, up_ref, down_ref):
    k = pl.program_id(0)
    pair, depth, offset = packed_place(GROUP - 1 - k)
    forcing = maps_ref[0, 0] * end_ref[0] - maps_ref[0, 1]
    out_ref[0] = forcing
    for m in range(4):

        @pl.when(m < 4 - pair)
        def _():
            up_ref[rows8(offset + depth - 8 * (m + 1)), :] = forcing[
                ROWS - 8 * (m + 1) : ROWS - 8 * m, :
            ]
            down_ref[rows8(offset + 8 * m), :] = forcing[8 * m : 8 * m + 8, :]


def forcing_of(info, maps, ends):
    columns = ends.shape[2]
    out = (PACKED, columns)
    block = pl.BlockSpec((1, ROWS, columns), lambda k, info: (k, 0, 0))
    return pl.pallas_call(
        forcing_kernel,
        grid_spec=pltpu.PrefetchScalarGridSpec(
            num_scalar_prefetch=1,
            grid=(GROUP,),
            in_specs=[
                pl.BlockSpec((1, 2, ROWS, columns), lambda k, info: (k ^ info[0], 0, 0, 0)),
                block,
            ],
            out_specs=[block, whole(out), whole(out)],
        ),
        out_shape=[jax.ShapeDtypeStruct(ends.shape, F32)]
        + [jax.ShapeDtypeStruct(out, F32)] * 2,
        compiler_params=params(16),
        cost_estimate=cost(1 << 20, 6 << 20),
        name="forcing",
    )(info, maps, ends)


def start_frame(frame, others, start_ref, low_ref, high_ref):
    edge = jnp.zeros((PAD, frame.shape[1]), F32)
    for ref in (frame,) + others:
        ref[0:PAD, :] = edge
        ref[PAD + FRAME : PAD + FRAME + PAD, :] = edge
    frame[PAD : PAD + HALO, :] = low_ref[...]
    frame[PAD + HALO : PAD + HALO + ROWS, :] = start_ref[...]
    frame[PAD + HALO + ROWS : PAD + FRAME, :] = high_ref[...]


def low_rows(m):
    first = PAD + HALO - 8 * (m + 1)
    return slice(first, first + 8)


def high_rows(m):
    first = PAD + HALO + ROWS + 8 * m
    return slice(first, first + 8)


def for_halo_blocks(pair, act):
    for m in range(4):
        if m == 0:
            act(m)
        else:
            pl.when(m < 4 - pair)(lambda m=m: act(m))


def add_frame(frame, pair, depth, offset, center, low_ref, high_ref, index):
    frame[PAD + HALO : PAD + HALO + ROWS, :] += center

    def act(m):
        frame[low_rows(m), :] += low_ref[index + (rows8(offset + depth - 8 * (m + 1)),)]
        frame[high_rows(m), :] += high_ref[index + (rows8(offset + 8 * m),)]

    for_halo_blocks(pair, act)


def forward_block(src, dst, first, u, v, mask):
    columns = src.shape[1]
    c = src[first : first + 8, :]
    n = src[first + 1 : first + 9, :]
    s = src[first - 1 : first + 7, :]
    e = pltpu.roll(c, columns - 1, 1)
    w = pltpu.roll(c, 1, 1)
    hu = 0.5 * u
    hv = 0.5 * v
    out = 0.6 * c + (0.1 - hu) * e + (0.1 + hu) * w + (0.1 - hv) * n + (0.1 + hv) * s
    if mask is not None:
        out = out * mask
    dst[first : first + 8, :] = out


def forward_kernel(
    info, start_ref, start_low, start_high, data_ref, data_low, data_high, out_ref, xa, xb
):
    low_mask = info[1].astype(F32)
    high_mask = info[2].astype(F32)
    start_frame(xa, (xb,), start_ref, start_low, start_high)

    def subwindow(i, carry):
        pair, depth, offset = packed_place(i)
        k = i ^ info[0]
        add_frame(xa, pair, depth, offset, data_ref[k, 0], data_low, data_high, (0,))
        for step in range(STEPS):
            src, dst = (xa, xb) if step % 2 == 0 else (xb, xa)
            for b in range(ROWS // 8):
                own = slice(8 * b, 8 * b + 8)
                u, v = data_ref[k, 1, own, :], data_ref[k, 2, own, :]
                forward_block(src, dst, PAD + HALO + 8 * b, u, v, None)

            def act(m):
                low = rows8(offset + depth - 8 * (m + 1))
                high = rows8(offset + 8 * m)
                u, v = data_low[1, low, :], data_low[2, low, :]
                forward_block(src, dst, low_rows(m).start, u, v, low_mask)
                u, v = data_high[1, high, :], data_high[2, high, :]
                forward_block(src, dst, high_rows(m).start, u, v, high_mask)

            for_halo_blocks(pair, act)
        out_ref[i] = xa[PAD + HALO : PAD + HALO + ROWS, :]
        return carry

    lax.fori_loop(0, GROUP, subwindow, 0)


def adjoint_block(src, dst, first, u, hv, mask):
    columns = src.shape[1]
    c = src[first : first + 8, :]
    n = src[first + 1 : first + 9, :]
    s = src[first - 1 : first + 7, :]
    hv_n = hv[first + 1 : first + 9, :]
    hv_s = hv[first - 1 : first + 7, :]
    spread = 0.1 * c
    flux = (0.5 * u) * c
    from_east = pltpu.roll(spread + flux, columns - 1, 1)
    from_west = pltpu.roll(spread - flux, 1, 1)
    out = 0.6 * c + from_east + from_west + (0.1 + hv_n) * n + (0.1 - hv_s) * s
    if mask is not None:
        out = out * mask
    dst[first : first + 8, :] = out


def adjoint_kernel(
    info,
    start_ref,
    start_low,
    start_high,
    forcing_ref,
    forcing_low,
    forcing_high,
    data_ref,
    data_low,
    data_high,
    out_ref,
    xa,
    xb,
    hv,
):
    low_mask = info[1].astype(F32)
    high_mask = info[2].astype(F32)
    start_frame(xa, (xb, hv), start_ref, start_low, start_high)

    def subwindow(i, carry):
        pair, depth, offset = packed_place(i)
        k = GROUP - 1 - i
        member = k ^ info[0]
        add_frame(xa, pair, depth, offset, forcing_ref[k], forcing_low, forcing_high, ())
        hv[PAD + HALO : PAD + HALO + ROWS, :] = 0.5 * data_ref[member, 2]

        def place_wind(m):
            low = rows8(offset + depth - 8 * (m + 1))
            high = rows8(offset + 8 * m)
            hv[low_rows(m), :] = 0.5 * data_low[1, low, :]
            hv[high_rows(m), :] = 0.5 * data_high[1, high, :]

        for_halo_blocks(pair, place_wind)
        for step in range(STEPS):
            src, dst = (xa, xb) if step % 2 == 0 else (xb, xa)
            for b in range(ROWS // 8):
                own = slice(8 * b, 8 * b + 8)
                adjoint_block(src, dst, PAD + HALO + 8 * b, data_ref[member, 1, own, :], hv, None)

            def act(m):
                low = rows8(offset + depth - 8 * (m + 1))
                high = rows8(offset + 8 * m)
                adjoint_block(src, dst, low_rows(m).start, data_low[0, low, :], hv, low_mask)
                adjoint_block(src, dst, high_rows(m).start, data_high[0, high, :], hv, high_mask)

            for_halo_blocks(pair, act)
        out_ref[k] = xa[PAD + HALO : PAD + HALO + ROWS, :]
        return carry

    lax.fori_loop(0, GROUP, subwindow, 0)


def forward_pass(info, start, data, data_halo):
    columns = data.shape[3]
    frame = pltpu.VMEM((FRAME + 2 * PAD, columns), F32)
    return pl.pallas_call(
        forward_kernel,
        in_specs=in_place(6),
        out_specs=pl.BlockSpec(memory_space=pltpu.VMEM),
        out_shape=jax.ShapeDtypeStruct((GROUP, ROWS, columns), F32),
        scratch_shapes=[frame] * 2,
        compiler_params=params(32, False),
        cost_estimate=cost(32 * 13 * 80 * columns, 8 << 20),
        name="tangent_pass",
    )(info, *start, data, *data_halo)


def adjoint_pass(info, start, forcing, forcing_halo, data, data_halo):
    columns = data.shape[3]
    frame = pltpu.VMEM((FRAME + 2 * PAD, columns), F32)
    return pl.pallas_call(
        adjoint_kernel,
        in_specs=in_place(9),
        out_specs=pl.BlockSpec(memory_space=pltpu.VMEM),
        out_shape=jax.ShapeDtypeStruct((GROUP, ROWS, columns), F32),
        scratch_shapes=[frame] * 3,
        compiler_params=params(32, False),
        cost_estimate=cost(32 * 13 * 80 * columns, 8 << 20),
        name="adjoint_pass",
    )(info, *start, forcing, *forcing_halo, data, *data_halo)


def split(value):
    high = value.astype(BF16)
    return high, (value - high.astype(F32)).astype(BF16)


def product(left, right):
    total = jnp.dot(left[0], right[1], preferred_element_type=F32)
    total = total + jnp.dot(left[1], right[0], preferred_element_type=F32)
    return total + jnp.dot(left[0], right[0], preferred_element_type=F32)


def zonal_kernel(info, adjoint_ref, deviation_ref, table_ref, out_ref, high, low):
    half = out_ref.shape[2]
    for o in range(GROUP):
        scaled = adjoint_ref[o] * deviation_ref[o ^ info[0]]
        high[o * ROWS : (o + 1) * ROWS, :], low[o * ROWS : (o + 1) * ROWS, :] = split(scaled)
    for part in range(2):
        lanes = slice(part * half, (part + 1) * half)
        result = product((high[...], low[...]), (table_ref[0, :, lanes], table_ref[1, :, lanes]))
        for o in range(GROUP):
            out_ref[2 * o + part] = result[o * ROWS : (o + 1) * ROWS, :]


def zonal(info, adjoint, deviation, table):
    vertical, rows, columns = deviation.shape
    out = (2 * vertical, rows, columns // 2)
    return pl.pallas_call(
        zonal_kernel,
        in_specs=in_place(3),
        out_specs=pl.BlockSpec(memory_space=pltpu.VMEM),
        scratch_shapes=[pltpu.VMEM((vertical * rows, columns), BF16)] * 2,
        out_shape=jax.ShapeDtypeStruct(out, F32),
        compiler_params=params(32, False),
        cost_estimate=cost(6 * vertical * rows * columns * columns, 6 << 20),
        name="zonal_forward",
    )(info, adjoint, deviation, table)


def meridional_kernel(bands_ref, spectrum_ref, table_ref, back_ref, out_ref):
    merid = product((table_ref[0], table_ref[1]), split(bands_ref[...])) * spectrum_ref[...]
    out_ref[...] = product((back_ref[0], back_ref[1]), split(merid))


def meridional(bands, spectrum, table, back):
    return pl.pallas_call(
        meridional_kernel,
        in_specs=in_place(4)[1:],
        out_specs=pl.BlockSpec(memory_space=pltpu.VMEM),
        out_shape=jax.ShapeDtypeStruct(bands.shape, F32),
        compiler_params=params(32, False),
        cost_estimate=cost(12 * bands.shape[0] * bands.size, 9 << 20),
        name="meridional",
    )(bands, spectrum, table, back)


def zonal_back_kernel(info, bands_ref, deviation_ref, increments_ref, table_ref, out_ref, high, low):
    half = bands_ref.shape[2]
    for o in range(GROUP):
        for part in range(2):
            rows = slice(o * ROWS, (o + 1) * ROWS)
            lanes = slice(part * half, (part + 1) * half)
            high[rows, lanes], low[rows, lanes] = split(bands_ref[2 * o + part])
    result = product((high[...], low[...]), (table_ref[0], table_ref[1]))
    for o in range(GROUP):
        v = o ^ info[0]
        rows = slice(o * ROWS, (o + 1) * ROWS)
        out_ref[v] = increments_ref[v] + deviation_ref[v] * result[rows, :]


def zonal_back(info, bands, deviation, increments, table):
    vertical, rows, columns = deviation.shape
    return pl.pallas_call(
        zonal_back_kernel,
        in_specs=in_place(4),
        out_specs=pl.BlockSpec(memory_space=pltpu.VMEM),
        scratch_shapes=[pltpu.VMEM((vertical * rows, columns), BF16)] * 2,
        out_shape=jax.ShapeDtypeStruct(deviation.shape, F32),
        compiler_params=params(32, False),
        cost_estimate=cost(6 * vertical * rows * columns * columns, 7 << 20),
        name="zonal_back",
    )(info, bands, deviation, increments, table)


def trade(pieces, count):
    swap = lambda piece, o: lax.ppermute(piece, "tm", [(i, i ^ o) for i in range(count)])
    return {o: swap(piece, o) if o else piece for o, piece in pieces.items()}


def in_order(pieces):
    return jnp.stack([pieces[o] for o in range(GROUP)])


def slab_rims(up, down, shift):
    tm, slabs = lax.axis_size("tm"), lax.axis_size("slab")
    at = lambda t, s: t * slabs + s
    pairs = [(t, t + shift) for t in range(tm) if 0 <= t + shift < tm]
    low = [(at(t, s), at(u, s + 1)) for t, u in pairs for s in range(slabs - 1)]
    high = [(at(t, s + 1), at(u, s)) for t, u in pairs for s in range(slabs - 1)]
    axes = ("tm", "slab")
    return lax.ppermute(up, axes, low), lax.ppermute(down, axes, high)


def next_group(state, shift):
    tm = lax.axis_size("tm")
    pairs = [(t, t + shift) for t in range(tm) if 0 <= t + shift < tm]
    middle = lax.ppermute(state, "tm", pairs)
    low, high = slab_rims(state[ROWS - HALO :], state[:HALO], shift)
    return middle, low, high


def body(increments, courant, deviation, spectrum, observed_cells, innovation, error_weights):
    tm, slabs = lax.axis_size("tm"), lax.axis_size("slab")
    place = lax.axis_index("tm") % GROUP
    slab = lax.axis_index("slab")
    info = jnp.stack([place, slab > 0, slab < slabs - 1]).astype(jnp.int32)
    state = increments[0].transpose(1, 0, 2)
    vertical, row_count, columns = state.shape
    winds = courant[0].transpose(1, 0, 2)
    pick = lambda array, o: lax.dynamic_index_in_dim(array, place ^ o, 0, keepdims=False)

    pieces = {
        o: jnp.concatenate([pick(state, o)[None], winds], axis=0) for o in (0,) + FAR_FIRST
    }
    data = in_order(trade(pieces, tm))
    parity = [list(range(c, slabs, 2)) for c in range(2)]
    waves = lax.all_gather(spectrum.T, "slab", axis_index_groups=parity, tiled=True)
    maps = scatter(observed_cells[0], error_weights[0], innovation[0], vertical, columns)
    data, waves, maps = lax.optimization_barrier((data, waves, maps))
    up, down = pack(info, data, 0, False)
    maps, up, down = lax.optimization_barrier((maps, up, down))
    data_halo = slab_rims(up, down, 0)
    moved = trade({o: pick(maps, o) for o in (0,) + Y_FIRST}, tm)

    zero = jnp.zeros((row_count, columns), F32)
    rim = jnp.zeros((HALO, columns), F32)
    ends = forward_pass(info, (zero, rim, rim), data, data_halo)
    start = next_group(ends[GROUP - 1], GROUP)
    late, start = lax.optimization_barrier((data, start))
    up, down = pack(info, late, 1, True)
    wind_halo = slab_rims(up, down, 0)
    ends = forward_pass(info, start, data, data_halo)

    forcing, up, down = forcing_of(info, in_order(moved), ends)
    forcing_halo = slab_rims(up, down, 0)
    starts = adjoint_pass(info, (zero, rim, rim), forcing, forcing_halo, data, wind_halo)
    starts = adjoint_pass(
        info, next_group(starts[0], -GROUP), forcing, forcing_halo, data, wind_halo
    )
    adjoint = in_order(trade({o: pick(starts, o) for o in (0,) + FAR_FIRST}, tm))

    half = columns // 2
    order = np.arange(columns).reshape(slabs // 2, 2, -1).transpose(1, 0, 2).reshape(-1)
    zonal_table = hartley_table(columns)[:, order]
    zonal_table, zonal_inverse = (
        jnp.asarray(split_table(table)) for table in (zonal_table, zonal_table.T)
    )
    cosine = cosine_table(slabs * row_count)
    merid_table = jnp.asarray(split_table(cosine))
    merid_back = jnp.asarray(split_table(cosine.T))
    deviation = deviation.transpose(1, 0, 2)
    waves = waves.T

    bands = zonal(info, adjoint, deviation, zonal_table)
    bands = lax.all_to_all(bands, "slab", 0, 0, tiled=True)
    bands = meridional(bands.reshape(slabs * row_count, half), waves, merid_table, merid_back)
    bands = lax.all_to_all(bands.reshape(slabs, row_count, half), "slab", 0, 0, tiled=True)
    gradient = zonal_back(info, bands, deviation, state, zonal_inverse)
    return gradient.transpose(1, 0, 2)[None]


def solution(mesh):
    in_specs = (
        P("tm", "slab", None, None),
        P("tm", "slab", None, None),
        P("slab", None, None),
        P(None, "slab"),
        P("tm", "slab"),
        P("tm", "slab"),
        P("tm", "slab"),
    )
    out_specs = P("tm", "slab", None, None)
    return jax.shard_map(body, mesh=mesh, in_specs=in_specs, out_specs=out_specs, check_vma=False)
```

```python
import functools
import math

import jax
import jax.numpy as jnp
import numpy as np
from jax import lax
from jax.experimental import pallas as pl
from jax.experimental.pallas import tpu as pltpu
from jax.sharding import PartitionSpec as P

STEPS = 4
GROUP = 8
HALO = 32
ROWS = 48
FRAME = ROWS + 2 * HALO
PAD = 8
PACKED = 160
Y_FIRST = (6, 7, 5, 4, 2, 3, 1)
F32 = jnp.float32
BF16 = jnp.bfloat16


def split_table(table):
    high = table.astype(jnp.bfloat16)
    low = (table - high.astype(np.float64)).astype(jnp.bfloat16)
    return np.stack([high, low])


def hartley_table(length):
    index = np.arange(length)
    angle = (index[:, None] * index[None, :] % length) * (2.0 * math.pi / length)
    return (np.cos(angle) + np.sin(angle)) / math.sqrt(length)


def cosine_table(length):
    index = np.arange(length)
    angle = ((2 * index[None, :] + 1) * index[:, None] % (4 * length)) * (math.pi / (2 * length))
    scales = np.where(index == 0, math.sqrt(1.0 / length), math.sqrt(2.0 / length))
    return scales[:, None] * np.cos(angle)


def params(megabytes, grid=True):
    return pltpu.CompilerParams(
        vmem_limit_bytes=megabytes * 1024 * 1024,
        dimension_semantics=("arbitrary",) if grid else None,
    )


def in_place(count):
    return [pl.BlockSpec(memory_space=pltpu.SMEM)] + [pl.BlockSpec(memory_space=pltpu.VMEM)] * count


def cost(flops, size):
    return pl.CostEstimate(flops=flops, bytes_accessed=size, transcendentals=0)


def whole(shape):
    return pl.BlockSpec(shape, lambda *_: (0,) * len(shape))


def packed_place(i):
    pair = lax.shift_right_logical(i, 1)
    depth = 32 - 8 * pair
    offset = 64 * pair - 8 * pair * (pair - 1) + (i & 1) * depth
    return pair, depth, offset


def rows8(start):
    return pl.ds(pl.multiple_of(start, 8), 8)


def scatter_kernel(row_ref, col_ref, w_ref, z_ref, *rest):
    before, (out_ref, acc) = rest[:-2], rest[-2:]
    step = pl.program_id(0)
    rows, cols = acc.shape[1], acc.shape[2]
    count = row_ref.shape[-1]

    @pl.when(step == 0)
    def _():
        if not before:
            acc[...] = jnp.zeros_like(acc)
        else:
            for v in range(rows // ROWS):
                for which in range(2):
                    acc[which, v * ROWS : (v + 1) * ROWS, :] = before[0][v, which]

    row_iota = lax.broadcasted_iota(jnp.int32, (rows, count), 0)
    col_iota = lax.broadcasted_iota(jnp.int32, (cols, count), 0)
    at_row = jnp.where(row_iota == row_ref[0], 1.0, 0.0).astype(BF16)
    at_col = jnp.where(col_iota == col_ref[0], 1.0, 0.0).astype(BF16)
    for which, ref in enumerate((w_ref, z_ref)):
        value = ref[0]
        high = value.astype(BF16)
        low = (value - high.astype(F32)).astype(BF16)
        for part in (high, low):
            acc[which] += lax.dot_general(
                at_row * part, at_col, (((1,), (1,)), ((), ())), preferred_element_type=F32
            )

    @pl.when(step == pl.num_programs(0) - 1)
    def _():
        for v in range(rows // ROWS):
            for which in range(2):
                out_ref[v, which] = acc[which, v * ROWS : (v + 1) * ROWS, :]


def scatter(cells, weights, innovation, vertical, columns):
    count = cells.shape[0]
    chunk = 1024
    line = cells // columns
    col = cells - line * columns
    row = (line % vertical) * ROWS + line // vertical
    shape = (count // chunk, 1, chunk)
    operands = [x.reshape(shape) for x in (row, col, weights, weights * innovation)]
    halves = count // chunk // 2
    out = (vertical, 2, ROWS, columns)
    maps = []
    for part in range(2):
        spec = pl.BlockSpec((1, 1, chunk), lambda i, part=part: (i + part * halves, 0, 0))
        maps = [
            pl.pallas_call(
                scatter_kernel,
                grid=(halves,),
                in_specs=[spec] * 4 + [whole(out)] * part,
                out_specs=whole(out),
                out_shape=jax.ShapeDtypeStruct(out, F32),
                scratch_shapes=[pltpu.VMEM((2, vertical * ROWS, columns), F32)],
                compiler_params=params(40),
                cost_estimate=cost(2 * 4 * count // 2 * vertical * ROWS * columns, 4 << 20),
                name=f"observation_maps_{part}",
            )(*operands, *maps)
        ]
    return maps[0]


def pack_kernel(skip, reverse, info, data_ref, up_ref, down_ref):
    k = pl.program_id(0)
    pair, depth, offset = packed_place(GROUP - 1 - k if reverse else k)
    for m in range(4):

        @pl.when(m < 4 - pair)
        def _():
            up_ref[:, rows8(offset + depth - 8 * (m + 1)), :] = data_ref[
                0, skip:, ROWS - 8 * (m + 1) : ROWS - 8 * m, :
            ]
            down_ref[:, rows8(offset + 8 * m), :] = data_ref[0, skip:, 8 * m : 8 * m + 8, :]


def pack(info, data, skip, reverse):
    parts, columns = data.shape[1], data.shape[3]
    out = (parts - skip, PACKED, columns)
    return pl.pallas_call(
        functools.partial(pack_kernel, skip, reverse),
        grid_spec=pltpu.PrefetchScalarGridSpec(
            num_scalar_prefetch=1,
            grid=(GROUP,),
            in_specs=[
                pl.BlockSpec((1, parts, ROWS, columns), lambda k, info: (k ^ info[0], 0, 0, 0))
            ],
            out_specs=[whole(out), whole(out)],
        ),
        out_shape=[jax.ShapeDtypeStruct(out, F32)] * 2,
        compiler_params=params(24),
        cost_estimate=cost(0, 6 << 20),
        name="pack_adjoint_halo" if reverse else "pack_halo",
    )(info, data)


def forcing_kernel(info, maps_ref, end_ref, out_ref, up_ref, down_ref):
    k = pl.program_id(0)
    pair, depth, offset = packed_place(GROUP - 1 - k)
    forcing = maps_ref[0, 0] * end_ref[0] - maps_ref[0, 1]
    out_ref[0] = forcing
    for m in range(4):

        @pl.when(m < 4 - pair)
        def _():
            up_ref[rows8(offset + depth - 8 * (m + 1)), :] = forcing[
                ROWS - 8 * (m + 1) : ROWS - 8 * m, :
            ]
            down_ref[rows8(offset + 8 * m), :] = forcing[8 * m : 8 * m + 8, :]


def forcing_of(info, maps, ends):
    columns = ends.shape[2]
    out = (PACKED, columns)
    block = pl.BlockSpec((1, ROWS, columns), lambda k, info: (k, 0, 0))
    return pl.pallas_call(
        forcing_kernel,
        grid_spec=pltpu.PrefetchScalarGridSpec(
            num_scalar_prefetch=1,
            grid=(GROUP,),
            in_specs=[
                pl.BlockSpec((1, 2, ROWS, columns), lambda k, info: (k ^ info[0], 0, 0, 0)),
                block,
            ],
            out_specs=[block, whole(out), whole(out)],
        ),
        out_shape=[jax.ShapeDtypeStruct(ends.shape, F32)]
        + [jax.ShapeDtypeStruct(out, F32)] * 2,
        compiler_params=params(16),
        cost_estimate=cost(1 << 20, 6 << 20),
        name="forcing",
    )(info, maps, ends)


def start_frame(frame, others, start_ref, low_ref, high_ref):
    edge = jnp.zeros((PAD, frame.shape[1]), F32)
    for ref in (frame,) + others:
        ref[0:PAD, :] = edge
        ref[PAD + FRAME : PAD + FRAME + PAD, :] = edge
    frame[PAD : PAD + HALO, :] = low_ref[...]
    frame[PAD + HALO : PAD + HALO + ROWS, :] = start_ref[...]
    frame[PAD + HALO + ROWS : PAD + FRAME, :] = high_ref[...]


def low_rows(m):
    first = PAD + HALO - 8 * (m + 1)
    return slice(first, first + 8)


def high_rows(m):
    first = PAD + HALO + ROWS + 8 * m
    return slice(first, first + 8)


def for_halo_blocks(pair, act):
    for m in range(4):
        if m == 0:
            act(m)
        else:
            pl.when(m < 4 - pair)(lambda m=m: act(m))


def add_frame(frame, pair, depth, offset, center, low_ref, high_ref, index):
    frame[PAD + HALO : PAD + HALO + ROWS, :] += center

    def act(m):
        frame[low_rows(m), :] += low_ref[index + (rows8(offset + depth - 8 * (m + 1)),)]
        frame[high_rows(m), :] += high_ref[index + (rows8(offset + 8 * m),)]

    for_halo_blocks(pair, act)


def forward_block(src, dst, first, u, v, mask):
    columns = src.shape[1]
    c = src[first : first + 8, :]
    n = src[first + 1 : first + 9, :]
    s = src[first - 1 : first + 7, :]
    e = pltpu.roll(c, columns - 1, 1)
    w = pltpu.roll(c, 1, 1)
    hu = 0.5 * u
    hv = 0.5 * v
    out = 0.6 * c + (0.1 - hu) * e + (0.1 + hu) * w + (0.1 - hv) * n + (0.1 + hv) * s
    if mask is not None:
        out = out * mask
    dst[first : first + 8, :] = out


def forward_kernel(
    info, start_ref, start_low, start_high, data_ref, data_low, data_high, out_ref, xa, xb
):
    low_mask = info[1].astype(F32)
    high_mask = info[2].astype(F32)
    start_frame(xa, (xb,), start_ref, start_low, start_high)

    def subwindow(i, carry):
        pair, depth, offset = packed_place(i)
        k = i ^ info[0]
        add_frame(xa, pair, depth, offset, data_ref[k, 0], data_low, data_high, (0,))
        for step in range(STEPS):
            src, dst = (xa, xb) if step % 2 == 0 else (xb, xa)
            for b in range(ROWS // 8):
                own = slice(8 * b, 8 * b + 8)
                u, v = data_ref[k, 1, own, :], data_ref[k, 2, own, :]
                forward_block(src, dst, PAD + HALO + 8 * b, u, v, None)

            def act(m):
                low = rows8(offset + depth - 8 * (m + 1))
                high = rows8(offset + 8 * m)
                u, v = data_low[1, low, :], data_low[2, low, :]
                forward_block(src, dst, low_rows(m).start, u, v, low_mask)
                u, v = data_high[1, high, :], data_high[2, high, :]
                forward_block(src, dst, high_rows(m).start, u, v, high_mask)

            for_halo_blocks(pair, act)
        out_ref[i] = xa[PAD + HALO : PAD + HALO + ROWS, :]
        return carry

    lax.fori_loop(0, GROUP, subwindow, 0)


def adjoint_block(src, dst, first, u, hv, mask):
    columns = src.shape[1]
    c = src[first : first + 8, :]
    n = src[first + 1 : first + 9, :]
    s = src[first - 1 : first + 7, :]
    hv_n = hv[first + 1 : first + 9, :]
    hv_s = hv[first - 1 : first + 7, :]
    spread = 0.1 * c
    flux = (0.5 * u) * c
    from_east = pltpu.roll(spread + flux, columns - 1, 1)
    from_west = pltpu.roll(spread - flux, 1, 1)
    out = 0.6 * c + from_east + from_west + (0.1 + hv_n) * n + (0.1 - hv_s) * s
    if mask is not None:
        out = out * mask
    dst[first : first + 8, :] = out


def adjoint_kernel(
    info,
    start_ref,
    start_low,
    start_high,
    forcing_ref,
    forcing_low,
    forcing_high,
    data_ref,
    data_low,
    data_high,
    out_ref,
    xa,
    xb,
    hv,
):
    low_mask = info[1].astype(F32)
    high_mask = info[2].astype(F32)
    start_frame(xa, (xb, hv), start_ref, start_low, start_high)

    def subwindow(i, carry):
        pair, depth, offset = packed_place(i)
        k = GROUP - 1 - i
        member = k ^ info[0]
        add_frame(xa, pair, depth, offset, forcing_ref[k], forcing_low, forcing_high, ())
        hv[PAD + HALO : PAD + HALO + ROWS, :] = 0.5 * data_ref[member, 2]

        def place_wind(m):
            low = rows8(offset + depth - 8 * (m + 1))
            high = rows8(offset + 8 * m)
            hv[low_rows(m), :] = 0.5 * data_low[1, low, :]
            hv[high_rows(m), :] = 0.5 * data_high[1, high, :]

        for_halo_blocks(pair, place_wind)
        for step in range(STEPS):
            src, dst = (xa, xb) if step % 2 == 0 else (xb, xa)
            for b in range(ROWS // 8):
                own = slice(8 * b, 8 * b + 8)
                adjoint_block(src, dst, PAD + HALO + 8 * b, data_ref[member, 1, own, :], hv, None)

            def act(m):
                low = rows8(offset + depth - 8 * (m + 1))
                high = rows8(offset + 8 * m)
                adjoint_block(src, dst, low_rows(m).start, data_low[0, low, :], hv, low_mask)
                adjoint_block(src, dst, high_rows(m).start, data_high[0, high, :], hv, high_mask)

            for_halo_blocks(pair, act)
        out_ref[k] = xa[PAD + HALO : PAD + HALO + ROWS, :]
        return carry

    lax.fori_loop(0, GROUP, subwindow, 0)


def forward_pass(info, start, data, data_halo):
    columns = data.shape[3]
    frame = pltpu.VMEM((FRAME + 2 * PAD, columns), F32)
    return pl.pallas_call(
        forward_kernel,
        in_specs=in_place(6),
        out_specs=pl.BlockSpec(memory_space=pltpu.VMEM),
        out_shape=jax.ShapeDtypeStruct((GROUP, ROWS, columns), F32),
        scratch_shapes=[frame] * 2,
        compiler_params=params(32, False),
        cost_estimate=cost(32 * 13 * 80 * columns, 8 << 20),
        name="tangent_pass",
    )(info, *start, data, *data_halo)


def adjoint_pass(info, start, forcing, forcing_halo, data, data_halo):
    columns = data.shape[3]
    frame = pltpu.VMEM((FRAME + 2 * PAD, columns), F32)
    return pl.pallas_call(
        adjoint_kernel,
        in_specs=in_place(9),
        out_specs=pl.BlockSpec(memory_space=pltpu.VMEM),
        out_shape=jax.ShapeDtypeStruct((GROUP, ROWS, columns), F32),
        scratch_shapes=[frame] * 3,
        compiler_params=params(32, False),
        cost_estimate=cost(32 * 13 * 80 * columns, 8 << 20),
        name="adjoint_pass",
    )(info, *start, forcing, *forcing_halo, data, *data_halo)


def split(value):
    high = value.astype(BF16)
    return high, (value - high.astype(F32)).astype(BF16)


def product(left, right):
    total = jnp.dot(left[0], right[1], preferred_element_type=F32)
    total = total + jnp.dot(left[1], right[0], preferred_element_type=F32)
    return total + jnp.dot(left[0], right[0], preferred_element_type=F32)


def zonal_kernel(info, adjoint_ref, deviation_ref, table_ref, out_ref, high, low):
    half = out_ref.shape[2]
    for o in range(GROUP):
        scaled = adjoint_ref[o] * deviation_ref[o ^ info[0]]
        high[o * ROWS : (o + 1) * ROWS, :], low[o * ROWS : (o + 1) * ROWS, :] = split(scaled)
    for part in range(2):
        lanes = slice(part * half, (part + 1) * half)
        result = product((high[...], low[...]), (table_ref[0, :, lanes], table_ref[1, :, lanes]))
        for o in range(GROUP):
            out_ref[2 * o + part] = result[o * ROWS : (o + 1) * ROWS, :]


def zonal(info, adjoint, deviation, table):
    vertical, rows, columns = deviation.shape
    out = (2 * vertical, rows, columns // 2)
    return pl.pallas_call(
        zonal_kernel,
        in_specs=in_place(3),
        out_specs=pl.BlockSpec(memory_space=pltpu.VMEM),
        scratch_shapes=[pltpu.VMEM((vertical * rows, columns), BF16)] * 2,
        out_shape=jax.ShapeDtypeStruct(out, F32),
        compiler_params=params(32, False),
        cost_estimate=cost(6 * vertical * rows * columns * columns, 6 << 20),
        name="zonal_forward",
    )(info, adjoint, deviation, table)


def meridional_kernel(bands_ref, spectrum_ref, table_ref, back_ref, out_ref):
    merid = product((table_ref[0], table_ref[1]), split(bands_ref[...])) * spectrum_ref[...]
    out_ref[...] = product((back_ref[0], back_ref[1]), split(merid))


def meridional(bands, spectrum, table, back):
    return pl.pallas_call(
        meridional_kernel,
        in_specs=in_place(4)[1:],
        out_specs=pl.BlockSpec(memory_space=pltpu.VMEM),
        out_shape=jax.ShapeDtypeStruct(bands.shape, F32),
        compiler_params=params(32, False),
        cost_estimate=cost(12 * bands.shape[0] * bands.size, 9 << 20),
        name="meridional",
    )(bands, spectrum, table, back)


def zonal_back_kernel(info, bands_ref, deviation_ref, increments_ref, table_ref, out_ref, high, low):
    half = bands_ref.shape[2]
    for o in range(GROUP):
        for part in range(2):
            rows = slice(o * ROWS, (o + 1) * ROWS)
            lanes = slice(part * half, (part + 1) * half)
            high[rows, lanes], low[rows, lanes] = split(bands_ref[2 * o + part])
    result = product((high[...], low[...]), (table_ref[0], table_ref[1]))
    for o in range(GROUP):
        v = o ^ info[0]
        rows = slice(o * ROWS, (o + 1) * ROWS)
        out_ref[v] = increments_ref[v] + deviation_ref[v] * result[rows, :]


def zonal_back(info, bands, deviation, increments, table):
    vertical, rows, columns = deviation.shape
    return pl.pallas_call(
        zonal_back_kernel,
        in_specs=in_place(4),
        out_specs=pl.BlockSpec(memory_space=pltpu.VMEM),
        scratch_shapes=[pltpu.VMEM((vertical * rows, columns), BF16)] * 2,
        out_shape=jax.ShapeDtypeStruct(deviation.shape, F32),
        compiler_params=params(32, False),
        cost_estimate=cost(6 * vertical * rows * columns * columns, 7 << 20),
        name="zonal_back",
    )(info, bands, deviation, increments, table)


def trade(pieces, count):
    swap = lambda piece, o: lax.ppermute(piece, "tm", [(i, i ^ o) for i in range(count)])
    return {o: swap(piece, o) if o else piece for o, piece in pieces.items()}


def in_order(pieces):
    return jnp.stack([pieces[o] for o in range(GROUP)])


def slab_rims(up, down, shift):
    tm, slabs = lax.axis_size("tm"), lax.axis_size("slab")
    at = lambda t, s: t * slabs + s
    pairs = [(t, t + shift) for t in range(tm) if 0 <= t + shift < tm]
    low = [(at(t, s), at(u, s + 1)) for t, u in pairs for s in range(slabs - 1)]
    high = [(at(t, s + 1), at(u, s)) for t, u in pairs for s in range(slabs - 1)]
    axes = ("tm", "slab")
    return lax.ppermute(up, axes, low), lax.ppermute(down, axes, high)


def next_group(state, shift):
    tm = lax.axis_size("tm")
    pairs = [(t, t + shift) for t in range(tm) if 0 <= t + shift < tm]
    middle = lax.ppermute(state, "tm", pairs)
    low, high = slab_rims(state[ROWS - HALO :], state[:HALO], shift)
    return middle, low, high


def body(increments, courant, deviation, spectrum, observed_cells, innovation, error_weights):
    tm, slabs = lax.axis_size("tm"), lax.axis_size("slab")
    place = lax.axis_index("tm") % GROUP
    slab = lax.axis_index("slab")
    info = jnp.stack([place, slab > 0, slab < slabs - 1]).astype(jnp.int32)
    state = increments[0].transpose(1, 0, 2)
    vertical, row_count, columns = state.shape
    winds = courant[0].transpose(1, 0, 2)
    pick = lambda array, o: lax.dynamic_index_in_dim(array, place ^ o, 0, keepdims=False)

    pieces = {
        o: jnp.concatenate([pick(state, o)[None], winds], axis=0) for o in (0,) + Y_FIRST
    }
    data = in_order(trade(pieces, tm))
    parity = [list(range(c, slabs, 2)) for c in range(2)]
    waves = lax.all_gather(spectrum.T, "slab", axis_index_groups=parity, tiled=True)
    maps = scatter(observed_cells[0], error_weights[0], innovation[0], vertical, columns)
    data, waves, maps = lax.optimization_barrier((data, waves, maps))
    up, down = pack(info, data, 0, False)
    maps, up, down = lax.optimization_barrier((maps, up, down))
    data_halo = slab_rims(up, down, 0)
    moved = trade({o: pick(maps, o) for o in (0,) + Y_FIRST}, tm)

    zero = jnp.zeros((row_count, columns), F32)
    rim = jnp.zeros((HALO, columns), F32)
    ends = forward_pass(info, (zero, rim, rim), data, data_halo)
    start = next_group(ends[GROUP - 1], GROUP)
    late, start = lax.optimization_barrier((data, start))
    up, down = pack(info, late, 1, True)
    wind_halo = slab_rims(up, down, 0)
    ends = forward_pass(info, start, data, data_halo)

    forcing, up, down = forcing_of(info, in_order(moved), ends)
    forcing_halo = slab_rims(up, down, 0)
    starts = adjoint_pass(info, (zero, rim, rim), forcing, forcing_halo, data, wind_halo)
    starts = adjoint_pass(
        info, next_group(starts[0], -GROUP), forcing, forcing_halo, data, wind_halo
    )
    adjoint = in_order(trade({o: pick(starts, o) for o in (0,) + Y_FIRST}, tm))

    half = columns // 2
    order = np.arange(columns).reshape(slabs // 2, 2, -1).transpose(1, 0, 2).reshape(-1)
    zonal_table = hartley_table(columns)[:, order]
    zonal_table, zonal_inverse = (
        jnp.asarray(split_table(table)) for table in (zonal_table, zonal_table.T)
    )
    cosine = cosine_table(slabs * row_count)
    merid_table = jnp.asarray(split_table(cosine))
    merid_back = jnp.asarray(split_table(cosine.T))
    deviation = deviation.transpose(1, 0, 2)
    waves = waves.T

    bands = zonal(info, adjoint, deviation, zonal_table)
    bands = lax.all_to_all(bands, "slab", 0, 0, tiled=True)
    bands = meridional(bands.reshape(slabs * row_count, half), waves, merid_table, merid_back)
    bands = lax.all_to_all(bands.reshape(slabs, row_count, half), "slab", 0, 0, tiled=True)
    gradient = zonal_back(info, bands, deviation, state, zonal_inverse)
    return gradient.transpose(1, 0, 2)[None]


def solution(mesh):
    in_specs = (
        P("tm", "slab", None, None),
        P("tm", "slab", None, None),
        P("slab", None, None),
        P(None, "slab"),
        P("tm", "slab"),
        P("tm", "slab"),
        P("tm", "slab"),
    )
    out_specs = P("tm", "slab", None, None)
    return jax.shard_map(body, mesh=mesh, in_specs=in_specs, out_specs=out_specs, check_vma=False)
```

```python
import functools
import math

import jax
import jax.numpy as jnp
import numpy as np
from jax import lax
from jax.experimental import pallas as pl
from jax.experimental.pallas import tpu as pltpu
from jax.sharding import PartitionSpec as P

STEPS = 4
GROUP = 8
HALO = 32
ROWS = 48
FRAME = ROWS + 2 * HALO
PAD = 8
PACKED = 160
Y_FIRST = (6, 7, 5, 4, 2, 3, 1)
F32 = jnp.float32
BF16 = jnp.bfloat16


def split_table(table):
    high = table.astype(jnp.bfloat16)
    low = (table - high.astype(np.float64)).astype(jnp.bfloat16)
    return np.stack([high, low])


def hartley_table(length):
    index = np.arange(length)
    angle = (index[:, None] * index[None, :] % length) * (2.0 * math.pi / length)
    return (np.cos(angle) + np.sin(angle)) / math.sqrt(length)


def cosine_table(length):
    index = np.arange(length)
    angle = ((2 * index[None, :] + 1) * index[:, None] % (4 * length)) * (math.pi / (2 * length))
    scales = np.where(index == 0, math.sqrt(1.0 / length), math.sqrt(2.0 / length))
    return scales[:, None] * np.cos(angle)


def params(megabytes, grid=True):
    return pltpu.CompilerParams(
        vmem_limit_bytes=megabytes * 1024 * 1024,
        dimension_semantics=("arbitrary",) if grid else None,
    )


def in_place(count):
    return [pl.BlockSpec(memory_space=pltpu.SMEM)] + [pl.BlockSpec(memory_space=pltpu.VMEM)] * count


def cost(flops, size):
    return pl.CostEstimate(flops=flops, bytes_accessed=size, transcendentals=0)


def whole(shape):
    return pl.BlockSpec(shape, lambda *_: (0,) * len(shape))


def packed_place(i):
    pair = lax.shift_right_logical(i, 1)
    depth = 32 - 8 * pair
    offset = 64 * pair - 8 * pair * (pair - 1) + (i & 1) * depth
    return pair, depth, offset


def rows8(start):
    return pl.ds(pl.multiple_of(start, 8), 8)


def scatter_kernel(row_ref, col_ref, w_ref, z_ref, *rest):
    before, (out_ref, acc) = rest[:-2], rest[-2:]
    step = pl.program_id(0)
    rows, cols = acc.shape[1], acc.shape[2]
    count = row_ref.shape[-1]

    @pl.when(step == 0)
    def _():
        if not before:
            acc[...] = jnp.zeros_like(acc)
        else:
            for v in range(rows // ROWS):
                for which in range(2):
                    acc[which, v * ROWS : (v + 1) * ROWS, :] = before[0][v, which]

    row_iota = lax.broadcasted_iota(jnp.int32, (rows, count), 0)
    col_iota = lax.broadcasted_iota(jnp.int32, (cols, count), 0)
    at_row = jnp.where(row_iota == row_ref[0], 1.0, 0.0).astype(BF16)
    at_col = jnp.where(col_iota == col_ref[0], 1.0, 0.0).astype(BF16)
    for which, ref in enumerate((w_ref, z_ref)):
        value = ref[0]
        high = value.astype(BF16)
        low = (value - high.astype(F32)).astype(BF16)
        for part in (high, low):
            acc[which] += lax.dot_general(
                at_row * part, at_col, (((1,), (1,)), ((), ())), preferred_element_type=F32
            )

    @pl.when(step == pl.num_programs(0) - 1)
    def _():
        for v in range(rows // ROWS):
            for which in range(2):
                out_ref[v, which] = acc[which, v * ROWS : (v + 1) * ROWS, :]


def scatter(cells, weights, innovation, vertical, columns):
    count = cells.shape[0]
    chunk = 1024
    line = cells // columns
    col = cells - line * columns
    row = (line % vertical) * ROWS + line // vertical
    shape = (count // chunk, 1, chunk)
    operands = [x.reshape(shape) for x in (row, col, weights, weights * innovation)]
    halves = count // chunk // 2
    out = (vertical, 2, ROWS, columns)
    maps = []
    for part in range(2):
        spec = pl.BlockSpec((1, 1, chunk), lambda i, part=part: (i + part * halves, 0, 0))
        maps = [
            pl.pallas_call(
                scatter_kernel,
                grid=(halves,),
                in_specs=[spec] * 4 + [whole(out)] * part,
                out_specs=whole(out),
                out_shape=jax.ShapeDtypeStruct(out, F32),
                scratch_shapes=[pltpu.VMEM((2, vertical * ROWS, columns), F32)],
                compiler_params=params(40),
                cost_estimate=cost(2 * 4 * count // 2 * vertical * ROWS * columns, 4 << 20),
                name=f"observation_maps_{part}",
            )(*operands, *maps)
        ]
    return maps[0]


def pack_kernel(skip, reverse, info, data_ref, up_ref, down_ref):
    k = pl.program_id(0)
    pair, depth, offset = packed_place(GROUP - 1 - k if reverse else k)
    for m in range(4):

        @pl.when(m < 4 - pair)
        def _():
            up_ref[:, rows8(offset + depth - 8 * (m + 1)), :] = data_ref[
                0, skip:, ROWS - 8 * (m + 1) : ROWS - 8 * m, :
            ]
            down_ref[:, rows8(offset + 8 * m), :] = data_ref[0, skip:, 8 * m : 8 * m + 8, :]


def pack(info, data, skip, reverse):
    parts, columns = data.shape[1], data.shape[3]
    out = (parts - skip, PACKED, columns)
    return pl.pallas_call(
        functools.partial(pack_kernel, skip, reverse),
        grid_spec=pltpu.PrefetchScalarGridSpec(
            num_scalar_prefetch=1,
            grid=(GROUP,),
            in_specs=[
                pl.BlockSpec((1, parts, ROWS, columns), lambda k, info: (k ^ info[0], 0, 0, 0))
            ],
            out_specs=[whole(out), whole(out)],
        ),
        out_shape=[jax.ShapeDtypeStruct(out, F32)] * 2,
        compiler_params=params(24),
        cost_estimate=cost(0, 6 << 20),
        name="pack_adjoint_halo" if reverse else "pack_halo",
    )(info, data)


def forcing_kernel(info, maps_ref, end_ref, out_ref, up_ref, down_ref):
    k = pl.program_id(0)
    pair, depth, offset = packed_place(GROUP - 1 - k)
    forcing = maps_ref[0, 0] * end_ref[0] - maps_ref[0, 1]
    out_ref[0] = forcing
    for m in range(4):

        @pl.when(m < 4 - pair)
        def _():
            up_ref[rows8(offset + depth - 8 * (m + 1)), :] = forcing[
                ROWS - 8 * (m + 1) : ROWS - 8 * m, :
            ]
            down_ref[rows8(offset + 8 * m), :] = forcing[8 * m : 8 * m + 8, :]


def forcing_of(info, maps, ends):
    columns = ends.shape[2]
    out = (PACKED, columns)
    block = pl.BlockSpec((1, ROWS, columns), lambda k, info: (k, 0, 0))
    return pl.pallas_call(
        forcing_kernel,
        grid_spec=pltpu.PrefetchScalarGridSpec(
            num_scalar_prefetch=1,
            grid=(GROUP,),
            in_specs=[
                pl.BlockSpec((1, 2, ROWS, columns), lambda k, info: (k ^ info[0], 0, 0, 0)),
                block,
            ],
            out_specs=[block, whole(out), whole(out)],
        ),
        out_shape=[jax.ShapeDtypeStruct(ends.shape, F32)]
        + [jax.ShapeDtypeStruct(out, F32)] * 2,
        compiler_params=params(16),
        cost_estimate=cost(1 << 20, 6 << 20),
        name="forcing",
    )(info, maps, ends)


def start_frame(frame, others, start_ref, low_ref, high_ref):
    edge = jnp.zeros((PAD, frame.shape[1]), F32)
    for ref in (frame,) + others:
        ref[0:PAD, :] = edge
        ref[PAD + FRAME : PAD + FRAME + PAD, :] = edge
    frame[PAD : PAD + HALO, :] = low_ref[...]
    frame[PAD + HALO : PAD + HALO + ROWS, :] = start_ref[...]
    frame[PAD + HALO + ROWS : PAD + FRAME, :] = high_ref[...]


def low_rows(m):
    first = PAD + HALO - 8 * (m + 1)
    return slice(first, first + 8)


def high_rows(m):
    first = PAD + HALO + ROWS + 8 * m
    return slice(first, first + 8)


def for_halo_blocks(pair, act):
    for m in range(4):
        if m == 0:
            act(m)
        else:
            pl.when(m < 4 - pair)(lambda m=m: act(m))


def add_frame(frame, pair, depth, offset, center, low_ref, high_ref, index):
    frame[PAD + HALO : PAD + HALO + ROWS, :] += center

    def act(m):
        frame[low_rows(m), :] += low_ref[index + (rows8(offset + depth - 8 * (m + 1)),)]
        frame[high_rows(m), :] += high_ref[index + (rows8(offset + 8 * m),)]

    for_halo_blocks(pair, act)


def forward_block(src, dst, first, u, v, mask):
    columns = src.shape[1]
    c = src[first : first + 8, :]
    n = src[first + 1 : first + 9, :]
    s = src[first - 1 : first + 7, :]
    e = pltpu.roll(c, columns - 1, 1)
    w = pltpu.roll(c, 1, 1)
    hu = 0.5 * u
    hv = 0.5 * v
    out = 0.6 * c + (0.1 - hu) * e + (0.1 + hu) * w + (0.1 - hv) * n + (0.1 + hv) * s
    if mask is not None:
        out = out * mask
    dst[first : first + 8, :] = out


def forward_kernel(
    info, start_ref, start_low, start_high, data_ref, data_low, data_high, out_ref, xa, xb
):
    low_mask = info[1].astype(F32)
    high_mask = info[2].astype(F32)
    start_frame(xa, (xb,), start_ref, start_low, start_high)

    def subwindow(i, carry):
        pair, depth, offset = packed_place(i)
        k = i ^ info[0]
        add_frame(xa, pair, depth, offset, data_ref[k, 0], data_low, data_high, (0,))
        for step in range(STEPS):
            src, dst = (xa, xb) if step % 2 == 0 else (xb, xa)
            for b in range(ROWS // 8):
                own = slice(8 * b, 8 * b + 8)
                u, v = data_ref[k, 1, own, :], data_ref[k, 2, own, :]
                forward_block(src, dst, PAD + HALO + 8 * b, u, v, None)

            def act(m):
                low = rows8(offset + depth - 8 * (m + 1))
                high = rows8(offset + 8 * m)
                u, v = data_low[1, low, :], data_low[2, low, :]
                forward_block(src, dst, low_rows(m).start, u, v, low_mask)
                u, v = data_high[1, high, :], data_high[2, high, :]
                forward_block(src, dst, high_rows(m).start, u, v, high_mask)

            for_halo_blocks(pair, act)
        out_ref[i] = xa[PAD + HALO : PAD + HALO + ROWS, :]
        return carry

    lax.fori_loop(0, GROUP, subwindow, 0)


def adjoint_block(src, dst, first, u, hv, mask):
    columns = src.shape[1]
    c = src[first : first + 8, :]
    n = src[first + 1 : first + 9, :]
    s = src[first - 1 : first + 7, :]
    hv_n = hv[first + 1 : first + 9, :]
    hv_s = hv[first - 1 : first + 7, :]
    spread = 0.1 * c
    flux = (0.5 * u) * c
    from_east = pltpu.roll(spread + flux, columns - 1, 1)
    from_west = pltpu.roll(spread - flux, 1, 1)
    out = 0.6 * c + from_east + from_west + (0.1 + hv_n) * n + (0.1 - hv_s) * s
    if mask is not None:
        out = out * mask
    dst[first : first + 8, :] = out


def adjoint_kernel(
    info,
    start_ref,
    start_low,
    start_high,
    forcing_ref,
    forcing_low,
    forcing_high,
    data_ref,
    data_low,
    data_high,
    out_ref,
    xa,
    xb,
    hv,
):
    low_mask = info[1].astype(F32)
    high_mask = info[2].astype(F32)
    start_frame(xa, (xb, hv), start_ref, start_low, start_high)

    def subwindow(i, carry):
        pair, depth, offset = packed_place(i)
        k = GROUP - 1 - i
        member = k ^ info[0]
        add_frame(xa, pair, depth, offset, forcing_ref[k], forcing_low, forcing_high, ())
        hv[PAD + HALO : PAD + HALO + ROWS, :] = 0.5 * data_ref[member, 2]

        def place_wind(m):
            low = rows8(offset + depth - 8 * (m + 1))
            high = rows8(offset + 8 * m)
            hv[low_rows(m), :] = 0.5 * data_low[1, low, :]
            hv[high_rows(m), :] = 0.5 * data_high[1, high, :]

        for_halo_blocks(pair, place_wind)
        for step in range(STEPS):
            src, dst = (xa, xb) if step % 2 == 0 else (xb, xa)
            for b in range(ROWS // 8):
                own = slice(8 * b, 8 * b + 8)
                adjoint_block(src, dst, PAD + HALO + 8 * b, data_ref[member, 1, own, :], hv, None)

            def act(m):
                low = rows8(offset + depth - 8 * (m + 1))
                high = rows8(offset + 8 * m)
                adjoint_block(src, dst, low_rows(m).start, data_low[0, low, :], hv, low_mask)
                adjoint_block(src, dst, high_rows(m).start, data_high[0, high, :], hv, high_mask)

            for_halo_blocks(pair, act)
        out_ref[k] = xa[PAD + HALO : PAD + HALO + ROWS, :]
        return carry

    lax.fori_loop(0, GROUP, subwindow, 0)


def forward_pass(info, start, data, data_halo):
    columns = data.shape[3]
    frame = pltpu.VMEM((FRAME + 2 * PAD, columns), F32)
    return pl.pallas_call(
        forward_kernel,
        in_specs=in_place(6),
        out_specs=pl.BlockSpec(memory_space=pltpu.VMEM),
        out_shape=jax.ShapeDtypeStruct((GROUP, ROWS, columns), F32),
        scratch_shapes=[frame] * 2,
        compiler_params=params(32, False),
        cost_estimate=cost(32 * 13 * 80 * columns, 8 << 20),
        name="tangent_pass",
    )(info, *start, data, *data_halo)


def adjoint_pass(info, start, forcing, forcing_halo, data, data_halo):
    columns = data.shape[3]
    frame = pltpu.VMEM((FRAME + 2 * PAD, columns), F32)
    return pl.pallas_call(
        adjoint_kernel,
        in_specs=in_place(9),
        out_specs=pl.BlockSpec(memory_space=pltpu.VMEM),
        out_shape=jax.ShapeDtypeStruct((GROUP, ROWS, columns), F32),
        scratch_shapes=[frame] * 3,
        compiler_params=params(32, False),
        cost_estimate=cost(32 * 13 * 80 * columns, 8 << 20),
        name="adjoint_pass",
    )(info, *start, forcing, *forcing_halo, data, *data_halo)


def split(value):
    high = value.astype(BF16)
    return high, (value - high.astype(F32)).astype(BF16)


def product(left, right):
    total = jnp.dot(left[0], right[1], preferred_element_type=F32)
    total = total + jnp.dot(left[1], right[0], preferred_element_type=F32)
    return total + jnp.dot(left[0], right[0], preferred_element_type=F32)


def zonal_kernel(info, adjoint_ref, deviation_ref, table_ref, out_ref, high, low):
    half = out_ref.shape[2]
    for o in range(GROUP):
        scaled = adjoint_ref[o] * deviation_ref[o ^ info[0]]
        high[o * ROWS : (o + 1) * ROWS, :], low[o * ROWS : (o + 1) * ROWS, :] = split(scaled)
    for part in range(2):
        lanes = slice(part * half, (part + 1) * half)
        result = product((high[...], low[...]), (table_ref[0, :, lanes], table_ref[1, :, lanes]))
        for o in range(GROUP):
            out_ref[2 * o + part] = result[o * ROWS : (o + 1) * ROWS, :]


def zonal(info, adjoint, deviation, table):
    vertical, rows, columns = deviation.shape
    out = (2 * vertical, rows, columns // 2)
    return pl.pallas_call(
        zonal_kernel,
        in_specs=in_place(3),
        out_specs=pl.BlockSpec(memory_space=pltpu.VMEM),
        scratch_shapes=[pltpu.VMEM((vertical * rows, columns), BF16)] * 2,
        out_shape=jax.ShapeDtypeStruct(out, F32),
        compiler_params=params(32, False),
        cost_estimate=cost(6 * vertical * rows * columns * columns, 6 << 20),
        name="zonal_forward",
    )(info, adjoint, deviation, table)


def meridional_kernel(bands_ref, spectrum_ref, table_ref, back_ref, out_ref):
    merid = product((table_ref[0], table_ref[1]), split(bands_ref[...])) * spectrum_ref[...]
    out_ref[...] = product((back_ref[0], back_ref[1]), split(merid))


def meridional(bands, spectrum, table, back):
    return pl.pallas_call(
        meridional_kernel,
        in_specs=in_place(4)[1:],
        out_specs=pl.BlockSpec(memory_space=pltpu.VMEM),
        out_shape=jax.ShapeDtypeStruct(bands.shape, F32),
        compiler_params=params(32, False),
        cost_estimate=cost(12 * bands.shape[0] * bands.size, 9 << 20),
        name="meridional",
    )(bands, spectrum, table, back)


def zonal_back_kernel(info, bands_ref, deviation_ref, increments_ref, table_ref, out_ref, high, low):
    half = bands_ref.shape[2]
    for o in range(GROUP):
        for part in range(2):
            rows = slice(o * ROWS, (o + 1) * ROWS)
            lanes = slice(part * half, (part + 1) * half)
            high[rows, lanes], low[rows, lanes] = split(bands_ref[2 * o + part])
    result = product((high[...], low[...]), (table_ref[0], table_ref[1]))
    for o in range(GROUP):
        v = o ^ info[0]
        rows = slice(o * ROWS, (o + 1) * ROWS)
        out_ref[v] = increments_ref[v] + deviation_ref[v] * result[rows, :]


def zonal_back(info, bands, deviation, increments, table):
    vertical, rows, columns = deviation.shape
    return pl.pallas_call(
        zonal_back_kernel,
        in_specs=in_place(4),
        out_specs=pl.BlockSpec(memory_space=pltpu.VMEM),
        scratch_shapes=[pltpu.VMEM((vertical * rows, columns), BF16)] * 2,
        out_shape=jax.ShapeDtypeStruct(deviation.shape, F32),
        compiler_params=params(32, False),
        cost_estimate=cost(6 * vertical * rows * columns * columns, 7 << 20),
        name="zonal_back",
    )(info, bands, deviation, increments, table)


def trade(pieces, count):
    swap = lambda piece, o: lax.ppermute(piece, "tm", [(i, i ^ o) for i in range(count)])
    return {o: swap(piece, o) if o else piece for o, piece in pieces.items()}


def in_order(pieces):
    whole_array = jnp.zeros((GROUP,) + pieces[0].shape, F32).at[0].set(pieces[0])
    for o in Y_FIRST:
        whole_array = whole_array.at[o].set(pieces[o])
    return whole_array


def slab_rims(up, down, shift):
    tm, slabs = lax.axis_size("tm"), lax.axis_size("slab")
    at = lambda t, s: t * slabs + s
    pairs = [(t, t + shift) for t in range(tm) if 0 <= t + shift < tm]
    low = [(at(t, s), at(u, s + 1)) for t, u in pairs for s in range(slabs - 1)]
    high = [(at(t, s + 1), at(u, s)) for t, u in pairs for s in range(slabs - 1)]
    axes = ("tm", "slab")
    return lax.ppermute(up, axes, low), lax.ppermute(down, axes, high)


def next_group(state, shift):
    tm = lax.axis_size("tm")
    pairs = [(t, t + shift) for t in range(tm) if 0 <= t + shift < tm]
    middle = lax.ppermute(state, "tm", pairs)
    low, high = slab_rims(state[ROWS - HALO :], state[:HALO], shift)
    return middle, low, high


def body(increments, courant, deviation, spectrum, observed_cells, innovation, error_weights):
    tm, slabs = lax.axis_size("tm"), lax.axis_size("slab")
    place = lax.axis_index("tm") % GROUP
    slab = lax.axis_index("slab")
    info = jnp.stack([place, slab > 0, slab < slabs - 1]).astype(jnp.int32)
    state = increments[0].transpose(1, 0, 2)
    vertical, row_count, columns = state.shape
    winds = courant[0].transpose(1, 0, 2)
    pick = lambda array, o: lax.dynamic_index_in_dim(array, place ^ o, 0, keepdims=False)

    pieces = {
        o: jnp.concatenate([pick(state, o)[None], winds], axis=0) for o in (0,) + Y_FIRST
    }
    data = in_order(trade(pieces, tm))
    parity = [list(range(c, slabs, 2)) for c in range(2)]
    waves = lax.all_gather(spectrum.T, "slab", axis_index_groups=parity, tiled=True)
    maps = scatter(observed_cells[0], error_weights[0], innovation[0], vertical, columns)
    data, waves, maps = lax.optimization_barrier((data, waves, maps))
    up, down = pack(info, data, 0, False)
    maps, up, down = lax.optimization_barrier((maps, up, down))
    data_halo = slab_rims(up, down, 0)
    moved = trade({o: pick(maps, o) for o in (0,) + Y_FIRST}, tm)

    zero = jnp.zeros((row_count, columns), F32)
    rim = jnp.zeros((HALO, columns), F32)
    ends = forward_pass(info, (zero, rim, rim), data, data_halo)
    start = next_group(ends[GROUP - 1], GROUP)
    late, start = lax.optimization_barrier((data, start))
    up, down = pack(info, late, 1, True)
    wind_halo = slab_rims(up, down, 0)
    ends = forward_pass(info, start, data, data_halo)

    forcing, up, down = forcing_of(info, in_order(moved), ends)
    forcing_halo = slab_rims(up, down, 0)
    starts = adjoint_pass(info, (zero, rim, rim), forcing, forcing_halo, data, wind_halo)
    starts = adjoint_pass(
        info, next_group(starts[0], -GROUP), forcing, forcing_halo, data, wind_halo
    )
    adjoint = in_order(trade({o: pick(starts, o) for o in (0,) + Y_FIRST}, tm))

    half = columns // 2
    order = np.arange(columns).reshape(slabs // 2, 2, -1).transpose(1, 0, 2).reshape(-1)
    zonal_table = hartley_table(columns)[:, order]
    zonal_table, zonal_inverse = (
        jnp.asarray(split_table(table)) for table in (zonal_table, zonal_table.T)
    )
    cosine = cosine_table(slabs * row_count)
    merid_table = jnp.asarray(split_table(cosine))
    merid_back = jnp.asarray(split_table(cosine.T))
    deviation = deviation.transpose(1, 0, 2)
    waves = waves.T

    bands = zonal(info, adjoint, deviation, zonal_table)
    bands = lax.all_to_all(bands, "slab", 0, 0, tiled=True)
    bands = meridional(bands.reshape(slabs * row_count, half), waves, merid_table, merid_back)
    bands = lax.all_to_all(bands.reshape(slabs, row_count, half), "slab", 0, 0, tiled=True)
    gradient = zonal_back(info, bands, deviation, state, zonal_inverse)
    return gradient.transpose(1, 0, 2)[None]


def solution(mesh):
    in_specs = (
        P("tm", "slab", None, None),
        P("tm", "slab", None, None),
        P("slab", None, None),
        P(None, "slab"),
        P("tm", "slab"),
        P("tm", "slab"),
        P("tm", "slab"),
    )
    out_specs = P("tm", "slab", None, None)
    return jax.shard_map(body, mesh=mesh, in_specs=in_specs, out_specs=out_specs, check_vma=False)
```
